256 devices in a mesh: blk: 256 (over y, x, z, core).
Axes of the slice: x: 4, y: 4, z: 8, core: 2. Of those that a mesh axis runs over, the one named last changes fastest.
Arguments:
- points: float32 [11, 524288], P(None, 'blk'), may hold values from -6 to 6
- values: float32 [16, 524288], P(None, 'blk'), may hold values from -0.046875 to 0.046875
- inverse_scale: float32 [11], replicated, may hold values from 0.08 to 0.4
Outputs:
- product: float32 [16, 524288], P(None, 'blk')
The draws below stay inside these ranges and needn't reach their ends.
All inputs are finite; a program needn't handle non-finite values.
Results may differ from the reference program's by a relative error of at most 0.0003.
Values sent between devices are 32-bit elements; how exact they have to be, the bound alone decides.
A program may use at most 256 MiB of HBM per device.

```python
import math
import jax
import jax.numpy as jnp
from jax import lax

FEAT = 11
RHS = 16
PTS_DEV = 2048
STEPS = 4
POINTS = 524288
N_BLK = 256


def shard_levels(own_key, dims, pieces, smallest, top_value):
    level, own = 1.0, jax.random.fold_in(own_key, 6)
    for dim, shards_of in pieces:
        heights = jnp.exp(jax.random.uniform(jax.random.fold_in(own, dim), (shards_of,), jnp.float32, smallest / len(pieces), top_value / len(pieces)))
        level = level * jnp.repeat(heights, dims[dim] // shards_of).reshape([-1 if axis == dim else 1 for axis in range(len(dims))])
    return level


def centred(rng, dims, scale, most, pieces=(), held_as=jnp.bfloat16):
    values = jax.random.normal(rng, dims, jnp.float32) * scale
    if len(pieces) > 0:
        values = shard_levels(rng, dims, pieces, -0.22, 0.18) * values
    return jnp.clip(values, min=-most, max=most).astype(held_as)


def setup_inputs(seed: int = 0) -> dict:
    seeds = jax.random.split(jax.random.key(seed), 4)
    points = centred(seeds[0], (FEAT, POINTS), 1.0, 6.0, ((1, 256),), jnp.float32)
    values = centred(seeds[1], (RHS, POINTS), (PTS_DEV * (2 * STEPS + 1)) ** -0.5, 0.046875, ((1, 256),), jnp.float32)
    inverse_scale = jnp.clip(jnp.exp(jax.random.uniform(seeds[2], (FEAT,), jnp.float32, math.log(0.08), math.log(0.4))), 0.08, 0.4)
    return dict(points=points, values=values, inverse_scale=inverse_scale)


def kernel_tile(left_pts, right_pts, inverse_scale):
    left_scaled = left_pts * inverse_scale[:, None]
    right_scaled = right_pts * inverse_scale[:, None]
    left_norm = lax.optimization_barrier(jnp.sum(left_scaled * left_scaled, axis=0))
    right_norm = lax.optimization_barrier(jnp.sum(right_scaled * right_scaled, axis=0))
    cross = lax.dot_general(left_scaled, right_scaled, (((0,), (0,)), ((), ())), precision=lax.Precision.HIGHEST, preferred_element_type=jnp.float32)
    squared = jnp.maximum(left_norm[:, None] + right_norm[None, :] - 2.0 * cross, 0.0)
    radius = jnp.sqrt(squared)
    root_five = jnp.sqrt(jnp.float32(5.0))
    return (1.0 + root_five * radius + 5.0 / 3.0 * squared) * jnp.exp(-root_five * radius)

def apply_tile(visitor_values, kernel_block):
    return lax.dot_general(visitor_values, kernel_block, (((1,), (1,)), ((), ())), precision=lax.Precision.HIGHEST, preferred_element_type=jnp.float32)

def reference(points, values, inverse_scale):
    blocks_x = points.reshape(FEAT, N_BLK, PTS_DEV).transpose(1, 0, 2)
    blocks_v = values.reshape(RHS, N_BLK, PTS_DEV).transpose(1, 0, 2)

    def one_block(block_index):
        home_points = blocks_x[block_index]
        summed = jnp.zeros((RHS, PTS_DEV), jnp.float32)
        for offset in range(-STEPS, STEPS + 1):
            other = ((block_index + offset + N_BLK) % N_BLK).astype(jnp.int32)
            kernel_block = kernel_tile(home_points, blocks_x[other], inverse_scale)
            summed = summed + apply_tile(blocks_v[other], kernel_block)
        return summed
    result = lax.map(one_block, jnp.arange(N_BLK, dtype=jnp.int32))
    return result.transpose(1, 0, 2).reshape(RHS, POINTS)
```

```python
import functools
import math

import jax
import jax.numpy as jnp
from jax import lax
from jax.experimental import pallas as pl
from jax.experimental.pallas import tpu as pltpu
from jax.sharding import PartitionSpec as P

STEPS = 4
LN2 = math.log(2.0)
SHIFT = 1.5 / LN2
BUMP = 0.75 / LN2**2
FACTOR = LN2**2 / 3.0
POINT_SCALE = math.sqrt(5.0) / LN2
LOW_SCALE = 2.0**14
VALUE_SCALE = 2.0**15
UNSCALE = 2.0**-29
MESH = pl.DeviceIdType.MESH

bf16, f32, f8 = jnp.bfloat16, jnp.float32, jnp.float8_e4m3fn
T = 256
OWN = 5


def dot(a, b, transposed=False):
    dims = (((1,), (1 if transposed else 0,)), ((), ()))
    return lax.dot_general(a, b, dims, preferred_element_type=f32)


def matern(s):
    s = jnp.maximum(s, 1e-30)
    t = s * lax.rsqrt(s)
    y = t + SHIFT
    return (y * y + BUMP) * jnp.exp2(-t)


def parts3(x):
    high = x.astype(bf16).astype(f32)
    rest = x - high
    middle = rest.astype(bf16).astype(f32)
    return high, middle, rest - middle


def body(
    n,
    scale_ref, points_ref, values_ref, out_ref,
    send_buf, recv_buf, home_t, b_ref, v_ref, v8_ref, ob_ref, ov_ref, ov8_ref,
    s_ref, kh_ref, kl_ref, oq, oq8, op, op8, ow, ow8, ret_send, ret_recv,
    send_sem, recv_sem, rsend_sem, rrecv_sem,
):
    me = lax.axis_index("blk")
    feat, pts = points_ref.shape
    rhs = values_ref.shape[0]
    nc = pts // T
    wide = pts + OWN * T

    def ahead(d):
        return lax.rem(me + d, n)

    def behind(d):
        return lax.rem(me + n - d, n)

    barrier = pltpu.get_barrier_semaphore()
    for d in range(1, STEPS + 1):
        pl.semaphore_signal(barrier, inc=1, device_id=(ahead(d),), device_id_type=MESH)
        pl.semaphore_signal(barrier, inc=1, device_id=(behind(d),), device_id_type=MESH)

    norm = jnp.zeros((1, pts), f32)
    for r in range(feat):
        w = points_ref[r : r + 1, :] * (scale_ref[r] * POINT_SCALE)
        send_buf[r : r + 1, :] = w
        norm = norm + w * w
    send_buf[feat : feat + 1, :] = norm
    send_buf[feat + 1 : feat + 2, :] = jnp.ones((1, pts), f32)
    send_buf[feat + 2 : 16, :] = jnp.zeros((14 - feat, pts), f32)
    send_buf[16:32, :] = values_ref[...] * FACTOR

    pl.semaphore_wait(barrier, 2 * STEPS)

    def block_copy(d):
        return pltpu.make_async_remote_copy(
            src_ref=send_buf,
            dst_ref=recv_buf.at[d - 1],
            send_sem=send_sem.at[d - 1],
            recv_sem=recv_sem.at[d - 1],
            device_id=(behind(d),),
            device_id_type=MESH,
        )

    def return_copy(d):
        return pltpu.make_async_remote_copy(
            src_ref=ret_send.at[d - 1],
            dst_ref=ret_recv.at[d - 1],
            send_sem=rsend_sem.at[d - 1],
            recv_sem=rrecv_sem.at[d - 1],
            device_id=(ahead(d),),
            device_id_type=MESH,
        )

    block_copy(1).start()
    block_copy(2).start()

    def right_side(x, c0, width, put):
        high, middle, low = parts3(x)
        for g, part in enumerate((high, middle, high, middle, low, high)):
            put(16 * g, part.astype(bf16), c0, width)

    def prepare(x, v, b, vv, v8):
        high, middle, low = (q.astype(bf16) for q in parts3(x))
        for g, part in enumerate((high, middle, high, middle, low, high)):
            b[16 * g : 16 * g + 16, :] = part
        vh = v.astype(bf16)
        vv[0:16, :] = vh
        vv[16:32, :] = (v - vh.astype(f32)).astype(bf16)
        v8[...] = jnp.concatenate([v * VALUE_SCALE, jnp.zeros_like(v)], 0).astype(f8)

    zero_rows = jnp.zeros((32, T), bf16)
    for c in range(nc):
        cols = pl.ds(c * T, T)
        x = send_buf[0:16, cols]
        prepare(x, send_buf[16:32, cols], ob_ref.at[:, cols], ov_ref.at[:, cols], ov8_ref.at[:, cols])
        ob_ref[96:128, cols] = zero_rows
        if c < OWN:
            again = pl.ds(pts + c * T, T)
            ob_ref[:, again] = ob_ref[:, cols]
            ov_ref[:, again] = ov_ref[:, cols]
            ov8_ref[:, again] = ov8_ref[:, cols]
        row = lax.broadcasted_iota(jnp.int32, (16, T), 0)
        y = jnp.where(
            row < feat,
            -2.0 * x,
            jnp.where(row == feat, 1.0, jnp.where(row == feat + 1, send_buf[feat : feat + 1, cols], 0.0)),
        )
        high, middle, low = parts3(y)
        nothing = jnp.zeros((32, T), f32)
        left = jnp.concatenate([high, high, middle, middle, high, low, nothing], 0)
        home_t[cols, :] = left.T.astype(bf16)
    for slot in range(2):
        b_ref[slot, 96:128, :] = jnp.zeros((32, pts), bf16)
    op[...] = jnp.zeros_like(op)
    op8[...] = jnp.zeros_like(op8)
    ow[...] = jnp.zeros_like(ow)
    ow8[...] = jnp.zeros_like(ow8)
    oq[...] = jnp.zeros_like(oq)
    oq8[...] = jnp.zeros_like(oq8)

    def chunk(i):
        return pl.ds(pl.multiple_of(i * T, T), T)

    def elementwise(j):
        for a in range(0, T, 32):
            rows, cols = slice(a, a + 32), slice(j * T, (j + 1) * T)
            k = matern(s_ref[rows, cols])
            high = k.astype(bf16)
            kh_ref[rows, cols] = high
            kl_ref[rows, cols] = ((k - high.astype(f32)) * LOW_SCALE).astype(f8)

    def apply(i, j, v, v8, cols, acc, acc8):
        tile = slice(j * T, (j + 1) * T)
        rows = chunk(i)
        kh, kl = kh_ref[:, tile], kl_ref[:, tile]
        op[:, rows] += dot(v[:, cols], kh, True)
        op8[:, rows] += dot(v8[0:16, cols], kl, True)
        if acc is not None:
            acc[:, cols] += dot(ov_ref[:, rows], kh)
            acc8[:, cols] += dot(ov8_ref[0:16, rows], kl)

    def own_cross(i, j):
        s_ref[:, j * T : (j + 1) * T] = dot(home_t[chunk(i), :], ob_ref[:, chunk(i + j)])

    def own_apply(i, j):
        both = 0 < j < OWN - 1
        apply(i, j, ov_ref, ov8_ref, chunk(i + j), ow if both else None, ow8 if both else None)

    def own_phase(first, last):
        for j in range(OWN):
            own_cross(first, j)
        for j in range(OWN):
            elementwise(j)
            own_cross(first + 1, j)

        def step(i, carry):
            following = jnp.minimum(i + 1, last)
            for j in range(OWN + 1):
                if j < OWN:
                    own_apply(i - 1, j)
                if j > 0:
                    elementwise(j - 1)
                    own_cross(following, j - 1)
            return carry

        lax.fori_loop(first + 1, last + 1, step, 0)
        for j in range(OWN):
            own_apply(last, j)

    own_phase(0, nc // 2 - 1)
    block_copy(3).start()
    block_copy(4).start()

    def take(d):
        block_copy(d + 1).wait_recv()
        slot = lax.rem(d, 2)
        for c in range(nc):
            cols = pl.ds(c * T, T)
            prepare(
                recv_buf[d, 0:16, cols], recv_buf[d, 16:32, cols],
                b_ref.at[slot, :, cols], v_ref.at[slot, :, cols], v8_ref.at[slot, :, cols],
            )

    def give_back(d):
        slot = lax.rem(d, 2)
        ret_send[d] = oq[slot, 0:16, :] + oq[slot, 16:32, :] + oq8[slot] * UNSCALE
        return_copy(d + 1).start()
        oq[slot] = jnp.zeros(oq.shape[1:], f32)
        oq8[slot] = jnp.zeros(oq8.shape[1:], f32)

    def cross(g, j):
        slot, i = lax.rem(g // nc, 2), lax.rem(g, nc)
        s_ref[:, j * T : (j + 1) * T] = dot(home_t[chunk(i), :], b_ref[slot, :, j * T : (j + 1) * T])

    def visit_apply(g, j):
        slot, i = lax.rem(g // nc, 2), lax.rem(g, nc)
        apply(i, j, v_ref.at[slot], v8_ref.at[slot], slice(j * T, (j + 1) * T), oq.at[slot], oq8.at[slot])

    take(0)
    for j in range(nc):
        cross(0, j)
    for j in range(nc):
        elementwise(j)
        cross(1, j)
    total = STEPS * nc

    def step(g, carry):
        i, d = lax.rem(g, nc), g // nc

        @pl.when(jnp.logical_and(i == nc - 1, d < STEPS - 1))
        def _():
            take(d + 1)

        @pl.when(jnp.logical_and(i == 1, d > 0))
        def _():
            give_back(d - 1)

        following = jnp.minimum(g + 1, total - 1)
        for j in range(nc + 1):
            if j < nc:
                visit_apply(g - 1, j)
            if j > 0:
                elementwise(j - 1)
                cross(following, j - 1)
        return carry

    lax.fori_loop(1, total, step, 0)
    for j in range(nc):
        visit_apply(total - 1, j)
    give_back(STEPS - 1)

    own_phase(nc // 2, nc - 1)

    for d in range(1, STEPS + 1):
        block_copy(d).wait_send()
        return_copy(d).wait()
    for c in range(nc):
        cols = pl.ds(c * T, T)
        low = op8[:, cols] + ow8[:, cols]
        sums = op[:, cols] + ow[:, cols]
        if c < OWN:
            low = low + ow8[:, pl.ds(pts + c * T, T)]
            sums = sums + ow[:, pl.ds(pts + c * T, T)]
        result = sums[0:16] + sums[16:32] + low * UNSCALE
        for d in range(STEPS):
            result = result + ret_recv[d, :, cols]
        out_ref[:, cols] = result


def per_device(n, points, values, inverse_scale):
    rhs, pts = values.shape
    wide = pts + OWN * T
    vmem = pl.BlockSpec(memory_space=pltpu.VMEM)
    return pl.pallas_call(
        functools.partial(body, n),
        out_shape=jax.ShapeDtypeStruct((rhs, pts), f32),
        in_specs=[pl.BlockSpec(memory_space=pltpu.SMEM), vmem, vmem],
        out_specs=vmem,
        scratch_shapes=[
            pltpu.VMEM((32, pts), f32),
            pltpu.VMEM((STEPS, 32, pts), f32),
            pltpu.VMEM((pts, 128), bf16),
            pltpu.VMEM((2, 128, pts), bf16),
            pltpu.VMEM((2, 32, pts), bf16),
            pltpu.VMEM((2, 32, pts), f8),
            pltpu.VMEM((128, wide), bf16),
            pltpu.VMEM((32, wide), bf16),
            pltpu.VMEM((32, wide), f8),
            pltpu.VMEM((T, pts), f32),
            pltpu.VMEM((T, pts), bf16),
            pltpu.VMEM((T, pts), f8),
            pltpu.VMEM((2, 32, pts), f32),
            pltpu.VMEM((2, 16, pts), f32),
            pltpu.VMEM((32, pts), f32),
            pltpu.VMEM((16, pts), f32),
            pltpu.VMEM((32, wide), f32),
            pltpu.VMEM((16, wide), f32),
            pltpu.VMEM((STEPS, rhs, pts), f32),
            pltpu.VMEM((STEPS, rhs, pts), f32),
            pltpu.SemaphoreType.DMA((STEPS,)),
            pltpu.SemaphoreType.DMA((STEPS,)),
            pltpu.SemaphoreType.DMA((STEPS,)),
            pltpu.SemaphoreType.DMA((STEPS,)),
        ],
        compiler_params=pltpu.CompilerParams(
            collective_id=0, has_side_effects=True, vmem_limit_bytes=48 << 20
        ),
        name="matern",
    )(inverse_scale, points, values)


def solution(mesh):
    placed = (P(None, "blk"), P(None, "blk"), P())
    return jax.shard_map(
        functools.partial(per_device, mesh.shape["blk"]),
        mesh=mesh, in_specs=placed, out_specs=P(None, "blk"), check_vma=False,
    )
```

```python
import functools
import math

import jax
import jax.numpy as jnp
from jax import lax
from jax.experimental import pallas as pl
from jax.experimental.pallas import tpu as pltpu
from jax.sharding import PartitionSpec as P

STEPS = 4
LN2 = math.log(2.0)
SHIFT = 1.5 / LN2
BUMP = 0.75 / LN2**2
FACTOR = LN2**2 / 3.0
POINT_SCALE = math.sqrt(5.0) / LN2
UP = 14
V8_MAX = 240.0
FIRST = 3
MESH = pl.DeviceIdType.MESH

bf16, f32, f8 = jnp.bfloat16, jnp.float32, jnp.float8_e4m3fn
T = 256
OWN_SLOT, NO_SLOT = 2, 3


def dot(a, b, transposed=False):
    dims = (((1,), (1 if transposed else 0,)), ((), ()))
    return lax.dot_general(a, b, dims, preferred_element_type=f32)


def matern(s):
    s = jnp.maximum(s, 1e-30)
    t = s * lax.rsqrt(s)
    y = t + SHIFT
    return (y * y + BUMP) * jnp.exp2(UP - t)


def parts3(x):
    high = x.astype(bf16).astype(f32)
    rest = x - high
    middle = rest.astype(bf16).astype(f32)
    return high, middle, rest - middle


def body(
    n,
    scale_ref, points_ref, values_ref, out_ref,
    send_buf, recv_buf, home_t, b_ref, v_ref, v8_ref,
    s_ref, kh0, kl0, kh1, kl1, oq, oq8, op, op8, ret_send, ret_recv,
    send_sem, recv_sem, rsend_sem, rrecv_sem,
):
    me = lax.axis_index("blk")
    feat, pts = points_ref.shape
    nc = pts // T
    own_steps = nc // 2 + 1
    total = own_steps + STEPS * nc
    high_refs, low_refs = (kh0, kh1), (kl0, kl1)

    def ahead(d):
        return lax.rem(me + d, n)

    def behind(d):
        return lax.rem(me + n - d, n)

    barrier = pltpu.get_barrier_semaphore()
    for d in range(1, STEPS + 1):
        pl.semaphore_signal(barrier, inc=1, device_id=(ahead(d),), device_id_type=MESH)
        pl.semaphore_signal(barrier, inc=1, device_id=(behind(d),), device_id_type=MESH)

    norm = jnp.zeros((1, pts), f32)
    for r in range(feat):
        w = points_ref[r : r + 1, :] * (scale_ref[r] * POINT_SCALE)
        send_buf[r : r + 1, :] = w
        norm = norm + w * w
    scaled = values_ref[...] * (FACTOR * 2.0**-UP)
    largest = jnp.max(jnp.max(jnp.abs(scaled), axis=0, keepdims=True), axis=1, keepdims=True)
    send_buf[feat : feat + 1, :] = norm
    send_buf[feat + 1 : feat + 2, :] = jnp.ones((1, pts), f32)
    send_buf[feat + 2 : feat + 3, :] = jnp.broadcast_to(
        jnp.maximum(largest, 1e-30) * (1.0 / V8_MAX), (1, pts)
    )
    send_buf[feat + 3 : 16, :] = jnp.zeros((13 - feat, pts), f32)
    send_buf[16:32, :] = scaled

    odd = lax.rem(me, 2)
    partner = me + 1 - 2 * odd

    def distance(k):
        return jnp.where(k == 0, 2, jnp.where(k == 1, 4, jnp.where(k == 2, 3, 1)))

    def block_copy(source, number, target, slot):
        return pltpu.make_async_remote_copy(
            src_ref=source,
            dst_ref=recv_buf.at[slot],
            send_sem=send_sem.at[number],
            recv_sem=recv_sem.at[slot],
            device_id=(target,),
            device_id_type=MESH,
        )

    def first_copy():
        return block_copy(send_buf, 0, behind(2), 0)

    def return_copy(k):
        return pltpu.make_async_remote_copy(
            src_ref=ret_send.at[k],
            dst_ref=ret_recv.at[distance(k) - 1],
            send_sem=rsend_sem.at[k],
            recv_sem=rrecv_sem.at[distance(k) - 1],
            device_id=(ahead(distance(k)),),
            device_id_type=MESH,
        )

    pl.semaphore_wait(barrier, 2 * STEPS)
    first_copy().start()

    @pl.when(odd == 1)
    def _():
        block_copy(send_buf, 3, partner, 3).start()

    def prepare(source, slot):
        for c in range(nc):
            cols = slice(c * T, (c + 1) * T)
            high, middle, low = (q.astype(bf16) for q in parts3(source[0:16, cols]))
            for g, part in enumerate((high, middle, high, middle, low, high)):
                b_ref[slot, 16 * g : 16 * g + 16, cols] = part
            v = source[16:32, cols]
            vh = v.astype(bf16)
            v_ref[slot, 0:16, cols] = vh
            v_ref[slot, 16:32, cols] = (v - vh.astype(f32)).astype(bf16)
            v8 = v * (1.0 / source[feat + 2 : feat + 3, cols])
            v8_ref[slot, :, cols] = jnp.concatenate([v8, jnp.zeros_like(v8)], 0).astype(f8)

    row = lax.broadcasted_iota(jnp.int32, (16, T), 0)
    nothing = jnp.zeros((32, T), f32)
    for c in range(nc):
        cols = slice(c * T, (c + 1) * T)
        y = jnp.where(
            row < feat,
            -2.0 * send_buf[0:16, cols],
            jnp.where(row == feat, 1.0, jnp.where(row == feat + 1, send_buf[feat : feat + 1, cols], 0.0)),
        )
        high, middle, low = parts3(y)
        left = jnp.concatenate([high, high, middle, middle, high, low, nothing], 0)
        home_t[cols, :] = left.T.astype(bf16)
    for slot in range(3):
        b_ref[slot, 96:128, :] = jnp.zeros((32, pts), bf16)
    prepare(send_buf, OWN_SLOT)
    for ref in (op, op8, oq, oq8):
        ref[...] = jnp.zeros_like(ref)

    def place(g):
        v = g - FIRST
        visit = jnp.logical_and(v >= 0, v < STEPS * nc)
        k = jnp.clip(v, 0, STEPS * nc - 1) // nc
        own = jnp.where(v < 0, g, g - STEPS * nc)
        slot = jnp.where(visit, lax.rem(k, 2), OWN_SLOT)
        offset = jnp.where(visit, jnp.clip(v, 0, STEPS * nc - 1) - k * nc, own)
        once = jnp.logical_or(own == 0, own == nc // 2)
        sums = jnp.where(visit, lax.rem(k, 2), jnp.where(once, NO_SLOT, OWN_SLOT))
        return slot, offset, sums

    def column(j, offset):
        return pl.ds(pl.multiple_of(lax.rem(j + offset, nc) * T, T), T)

    def cross(where, j):
        slot, offset, _ = where
        s_ref[:, j * T : (j + 1) * T] = dot(
            home_t[j * T : (j + 1) * T, :], b_ref[slot, :, column(j, offset)]
        )

    def elementwise(parity, j):
        for a in range(0, T, 32):
            rows, cols = slice(a, a + 32), slice(j * T, (j + 1) * T)
            k = matern(s_ref[rows, cols])
            high = k.astype(bf16)
            high_refs[parity][rows, cols] = high
            low_refs[parity][rows, cols] = (k - high.astype(f32)).astype(f8)

    def apply(where, parity, j):
        slot, offset, sums = where
        tile, cols = slice(j * T, (j + 1) * T), column(j, offset)
        kh, kl = high_refs[parity][:, tile], low_refs[parity][:, tile]
        op[:, tile] += dot(v_ref[slot, :, cols], kh, True)
        oq[sums, :, cols] += dot(v_ref[OWN_SLOT, :, tile], kh)
        op8[:, tile] += dot(v8_ref[slot, 0:16, cols], kl, True)
        oq8[sums, :, cols] += dot(v8_ref[OWN_SLOT, 0:16, tile], kl)

    def take(k):
        block_copy(send_buf, 0, partner, k).wait_recv()

        @pl.when(k == 0)
        def _():
            block_copy(recv_buf.at[0], 1, behind(2), 1).start()
            block_copy(recv_buf.at[0], 2, partner, 3 - odd).start()

        @pl.when(jnp.logical_and(k == 1, odd == 0))
        def _():
            block_copy(recv_buf.at[1], 3, partner, 2).start()

        prepare(recv_buf.at[k], lax.rem(k, 2))

    def settle(scale):
        op[0:16, :] += op8[...] * scale
        op8[...] = jnp.zeros_like(op8)

    def give_back(k):
        slot = lax.rem(k, 2)
        scale = send_buf[feat + 2 : feat + 3, :]
        ret_send[k] = oq[slot, 0:16, :] + oq[slot, 16:32, :] + oq8[slot] * scale
        return_copy(k).start()
        oq[slot] = jnp.zeros(oq.shape[1:], f32)
        oq8[slot] = jnp.zeros(oq8.shape[1:], f32)
        settle(recv_buf[k, feat + 2 : feat + 3, :])

    def events(g):
        due = g - FIRST + 1

        @pl.when(jnp.logical_and(lax.rem(due, nc) == 0, due < STEPS * nc))
        def _():
            take(due // nc)

        done = g - FIRST - 1

        @pl.when(done == 0)
        def _():
            settle(send_buf[feat + 2 : feat + 3, :])

        @pl.when(jnp.logical_and(lax.rem(done, nc) == 0, done > 0))
        def _():
            give_back(done // nc - 1)

    def work(g, parity):
        before, after = place(g - 1), place(jnp.minimum(g + 1, total - 1))
        for j in range(nc):
            elementwise(parity, j)
            cross(after, j)
            apply(before, 1 - parity, j)

    start, second = place(jnp.int32(0)), place(jnp.int32(1))
    for j in range(nc):
        cross(start, j)
    for j in range(nc):
        elementwise(0, j)
        cross(second, j)

    def pair(h, carry):
        g = 2 * h + 1
        work(g, 1)
        events(g + 1)
        work(g + 1, 0)
        return carry

    lax.fori_loop(0, (total - 1) // 2, pair, 0)
    final = place(jnp.int32(total - 1))
    for j in range(nc):
        apply(final, 0, j)

    for k in range(STEPS):
        block_copy(send_buf, k, partner, 0).wait_send()
        return_copy(k).wait_send()
        return_copy(k).wait_recv()
    for c in range(nc):
        cols = slice(c * T, (c + 1) * T)
        low = op8[:, cols] + oq8[OWN_SLOT, :, cols]
        sums = op[:, cols] + oq[OWN_SLOT, :, cols]
        result = sums[0:16] + sums[16:32] + low * send_buf[feat + 2 : feat + 3, cols]
        for k in range(STEPS):
            result = result + ret_recv[k, :, cols]
        out_ref[:, cols] = result


def per_device(n, points, values, inverse_scale):
    rhs, pts = values.shape
    vmem = pl.BlockSpec(memory_space=pltpu.VMEM)
    return pl.pallas_call(
        functools.partial(body, n),
        out_shape=jax.ShapeDtypeStruct((rhs, pts), f32),
        in_specs=[pl.BlockSpec(memory_space=pltpu.SMEM), vmem, vmem],
        out_specs=vmem,
        scratch_shapes=[
            pltpu.VMEM((32, pts), f32),
            pltpu.VMEM((STEPS, 32, pts), f32),
            pltpu.VMEM((pts, 128), bf16),
            pltpu.VMEM((3, 128, pts), bf16),
            pltpu.VMEM((3, 32, pts), bf16),
            pltpu.VMEM((3, 32, pts), f8),
            pltpu.VMEM((T, pts), f32),
            pltpu.VMEM((T, pts), bf16),
            pltpu.VMEM((T, pts), f8),
            pltpu.VMEM((T, pts), bf16),
            pltpu.VMEM((T, pts), f8),
            pltpu.VMEM((4, 32, pts), f32),
            pltpu.VMEM((4, 16, pts), f32),
            pltpu.VMEM((32, pts), f32),
            pltpu.VMEM((16, pts), f32),
            pltpu.VMEM((STEPS, rhs, pts), f32),
            pltpu.VMEM((STEPS, rhs, pts), f32),
            pltpu.SemaphoreType.DMA((STEPS,)),
            pltpu.SemaphoreType.DMA((STEPS,)),
            pltpu.SemaphoreType.DMA((STEPS,)),
            pltpu.SemaphoreType.DMA((STEPS,)),
        ],
        compiler_params=pltpu.CompilerParams(
            collective_id=0, has_side_effects=True, vmem_limit_bytes=48 << 20
        ),
        name="matern",
    )(inverse_scale, points, values)


def solution(mesh):
    placed = (P(None, "blk"), P(None, "blk"), P())
    return jax.shard_map(
        functools.partial(per_device, mesh.shape["blk"]),
        mesh=mesh, in_specs=placed, out_specs=P(None, "blk"), check_vma=False,
    )
```

```python
import functools
import math

import jax
import jax.numpy as jnp
from jax import lax
from jax.experimental import pallas as pl
from jax.experimental.pallas import tpu as pltpu
from jax.sharding import PartitionSpec as P

STEPS = 4
LN2 = math.log(2.0)
SHIFT = 1.5 / LN2
BUMP = 0.75 / LN2**2
FACTOR = LN2**2 / 3.0
POINT_SCALE = math.sqrt(5.0) / LN2
UP = 14
V8_MAX = 240.0
MESH = pl.DeviceIdType.MESH

bf16, f32, f8 = jnp.bfloat16, jnp.float32, jnp.float8_e4m3fn
T = 256
OWN_SLOT, NO_SLOT = 2, 3


def dot(a, b, transposed=False):
    dims = (((1,), (1 if transposed else 0,)), ((), ()))
    return lax.dot_general(a, b, dims, preferred_element_type=f32)


def matern(s):
    s = jnp.maximum(s, 1e-30)
    t = s * lax.rsqrt(s)
    y = t + SHIFT
    return (y * y + BUMP) * jnp.exp2(UP - t)


def parts3(x):
    high = x.astype(bf16).astype(f32)
    rest = x - high
    middle = rest.astype(bf16).astype(f32)
    return high, middle, rest - middle


def body(
    n,
    scale_ref, points_ref, values_ref, out_ref,
    send_buf, recv_buf, home_t, b_ref, v_ref, v8_ref,
    s_ref, kh0, kl0, kh1, kl1, oq, oq8, op, op8, ret_send, ret_recv,
    points_buf, values_buf, send_sem, recv_sem, rsend_sem, rrecv_sem, load_sem,
):
    me = lax.axis_index("blk")
    loads = [
        pltpu.make_async_copy(points_ref, points_buf, load_sem.at[0]),
        pltpu.make_async_copy(values_ref, values_buf, load_sem.at[1]),
    ]
    for load in loads:
        load.start()
    feat, pts = points_ref.shape
    nc = pts // T
    own_steps = nc // 2 + 1
    total = own_steps + STEPS * nc
    first = own_steps
    high_refs, low_refs = (kh0, kh1), (kl0, kl1)

    def ahead(d):
        return lax.rem(me + n - d, n)

    def behind(d):
        return lax.rem(me + d, n)

    odd = 1 - lax.rem(me, 2)
    partner = me - 1 + 2 * odd
    barrier = pltpu.get_barrier_semaphore()
    for other in (ahead(2), partner):
        pl.semaphore_signal(barrier, inc=1, device_id=(other,), device_id_type=MESH)

    for load in loads:
        load.wait()
    norm = jnp.zeros((1, pts), f32)
    for r in range(feat):
        w = points_buf[r : r + 1, :] * (scale_ref[r] * POINT_SCALE)
        send_buf[r : r + 1, :] = w
        norm = norm + w * w
    scaled = values_buf[...] * (FACTOR * 2.0**-UP)
    largest = jnp.max(jnp.max(jnp.abs(scaled), axis=0, keepdims=True), axis=1, keepdims=True)
    send_buf[feat : feat + 1, :] = norm
    send_buf[feat + 1 : feat + 2, :] = jnp.ones((1, pts), f32)
    send_buf[feat + 2 : feat + 3, :] = jnp.broadcast_to(
        jnp.maximum(largest, 1e-30) * (1.0 / V8_MAX), (1, pts)
    )
    send_buf[feat + 3 : 16, :] = jnp.zeros((13 - feat, pts), f32)
    send_buf[16:32, :] = scaled


    def distance(k):
        even_order = jnp.where(k == 0, 1, jnp.where(k == 1, 3, jnp.where(k == 2, 4, 2)))
        odd_order = jnp.where(k == 0, 2, jnp.where(k == 1, 4, jnp.where(k == 2, 3, 1)))
        return jnp.where(odd == 1, odd_order, even_order)

    def block_copy(source, number, target, slot):
        return pltpu.make_async_remote_copy(
            src_ref=source,
            dst_ref=recv_buf.at[slot],
            send_sem=send_sem.at[number],
            recv_sem=recv_sem.at[slot],
            device_id=(target,),
            device_id_type=MESH,
        )

    def first_copy():
        return block_copy(send_buf, 0, behind(2), 3 - 3 * odd)

    def relay(source):
        block_copy(source, 1, behind(2), 2 - odd).start()
        block_copy(source, 2, partner, 3 - 2 * odd).start()

    def arrived(slot):
        block_copy(send_buf, 0, partner, slot).wait_recv()

    def return_copy(k):
        return pltpu.make_async_remote_copy(
            src_ref=ret_send.at[k],
            dst_ref=ret_recv.at[distance(k) - 1],
            send_sem=rsend_sem.at[k],
            recv_sem=rrecv_sem.at[distance(k) - 1],
            device_id=(ahead(distance(k)),),
            device_id_type=MESH,
        )

    pl.semaphore_wait(barrier, 2)

    @pl.when(odd == 1)
    def _():
        first_copy().start()
        block_copy(send_buf, 3, partner, 0).start()

    def prepare(source, slot):
        for c in range(nc):
            cols = slice(c * T, (c + 1) * T)
            high, middle, low = (q.astype(bf16) for q in parts3(source[0:16, cols]))
            for g, part in enumerate((high, middle, high, middle, low, high)):
                b_ref[slot, 16 * g : 16 * g + 16, cols] = part
            v = source[16:32, cols]
            vh = v.astype(bf16)
            v_ref[slot, 0:16, cols] = vh
            v_ref[slot, 16:32, cols] = (v - vh.astype(f32)).astype(bf16)
            v8 = v * (1.0 / source[feat + 2 : feat + 3, cols])
            v8_ref[slot, :, cols] = jnp.concatenate([v8, jnp.zeros_like(v8)], 0).astype(f8)

    row = lax.broadcasted_iota(jnp.int32, (16, T), 0)
    nothing = jnp.zeros((32, T), f32)
    for c in range(nc):
        cols = slice(c * T, (c + 1) * T)
        y = jnp.where(
            row < feat,
            -2.0 * send_buf[0:16, cols],
            jnp.where(row == feat, 1.0, jnp.where(row == feat + 1, send_buf[feat : feat + 1, cols], 0.0)),
        )
        high, middle, low = parts3(y)
        left = jnp.concatenate([high, high, middle, middle, high, low, nothing], 0)
        home_t[cols, :] = left.T.astype(bf16)
    for slot in range(3):
        b_ref[slot, 96:128, :] = jnp.zeros((32, pts), bf16)
    prepare(send_buf, OWN_SLOT)
    for ref in (op, op8, oq, oq8):
        ref[...] = jnp.zeros_like(ref)

    def place(g):
        v = g - first
        visit = jnp.logical_and(v >= 0, v < STEPS * nc)
        k = jnp.clip(v, 0, STEPS * nc - 1) // nc
        own = jnp.where(v < 0, g, g - STEPS * nc)
        slot = jnp.where(visit, lax.rem(k, 2), OWN_SLOT)
        offset = jnp.where(visit, jnp.clip(v, 0, STEPS * nc - 1) - k * nc, own)
        once = jnp.logical_or(own == 0, own == nc // 2)
        sums = jnp.where(visit, lax.rem(k, 2), jnp.where(once, NO_SLOT, OWN_SLOT))
        return slot, offset, sums

    def column(j, offset):
        return pl.ds(pl.multiple_of(lax.rem(j + offset, nc) * T, T), T)

    def cross(where, j):
        slot, offset, _ = where
        s_ref[:, j * T : (j + 1) * T] = dot(
            home_t[j * T : (j + 1) * T, :], b_ref[slot, :, column(j, offset)]
        )

    def elementwise(parity, j):
        for a in range(0, T, 32):
            rows, cols = slice(a, a + 32), slice(j * T, (j + 1) * T)
            k = matern(s_ref[rows, cols])
            high = k.astype(bf16)
            high_refs[parity][rows, cols] = high
            low_refs[parity][rows, cols] = (k - high.astype(f32)).astype(f8)

    def apply(where, parity, j):
        slot, offset, sums = where
        tile, cols = slice(j * T, (j + 1) * T), column(j, offset)
        kh, kl = high_refs[parity][:, tile], low_refs[parity][:, tile]
        op[:, tile] += dot(v_ref[slot, :, cols], kh, True)
        oq[sums, :, cols] += dot(v_ref[OWN_SLOT, :, tile], kh)
        op8[:, tile] += dot(v8_ref[slot, 0:16, cols], kl, True)
        oq8[sums, :, cols] += dot(v8_ref[OWN_SLOT, 0:16, tile], kl)

    def take(k):
        @pl.when(jnp.logical_or(odd == 1, k < 2))
        def _():
            arrived(k)

        @pl.when(jnp.logical_and(odd == 1, k == 0))
        def _():
            relay(recv_buf.at[0])

        prepare(recv_buf.at[k], lax.rem(k, 2))

    def settle(scale):
        op[0:16, :] += op8[...] * scale
        op8[...] = jnp.zeros_like(op8)

    def give_back(k):
        slot = lax.rem(k, 2)
        scale = send_buf[feat + 2 : feat + 3, :]
        ret_send[k] = oq[slot, 0:16, :] + oq[slot, 16:32, :] + oq8[slot] * scale
        return_copy(k).start()
        oq[slot] = jnp.zeros(oq.shape[1:], f32)
        oq8[slot] = jnp.zeros(oq8.shape[1:], f32)
        settle(recv_buf[k, feat + 2 : feat + 3, :])

    def events(g):
        @pl.when(jnp.logical_and(g == 2, odd == 0))
        def _():
            first_copy().start()

        due = g - first + 1

        @pl.when(jnp.logical_and(lax.rem(due, nc) == 0, jnp.logical_and(due >= 0, due < STEPS * nc)))
        def _():
            take(due // nc)

        @pl.when(jnp.logical_and(g == 6, odd == 0))
        def _():
            arrived(3)
            relay(recv_buf.at[3])

        @pl.when(jnp.logical_and(g == 14, odd == 0))
        def _():
            arrived(2)
            block_copy(recv_buf.at[2], 3, partner, 2).start()

        done = g - first - 1

        @pl.when(done == 0)
        def _():
            settle(send_buf[feat + 2 : feat + 3, :])

        @pl.when(jnp.logical_and(lax.rem(done, nc) == 0, done > 0))
        def _():
            give_back(done // nc - 1)

    def work(g, parity):
        before, after = place(g - 1), place(jnp.minimum(g + 1, total - 1))
        for j in range(nc):
            elementwise(parity, j)
            cross(after, j)
            apply(before, 1 - parity, j)

    start, second = place(jnp.int32(0)), place(jnp.int32(1))
    for j in range(nc):
        cross(start, j)
    for j in range(nc):
        elementwise(0, j)
        cross(second, j)
    def pair(h, carry):
        g = 2 * h + 1
        work(g, 1)
        events(g + 1)
        work(g + 1, 0)
        return carry

    lax.fori_loop(0, (total - 1) // 2, pair, 0)
    final = place(jnp.int32(total - 1))
    for j in range(nc):
        apply(final, 0, j)

    give_back(STEPS - 1)

    for k in range(STEPS):
        block_copy(send_buf, k, partner, 0).wait_send()
        return_copy(k).wait_send()
        return_copy(k).wait_recv()
    for c in range(nc):
        cols = slice(c * T, (c + 1) * T)
        low = op8[:, cols] + oq8[OWN_SLOT, :, cols]
        sums = op[:, cols] + oq[OWN_SLOT, :, cols]
        result = sums[0:16] + sums[16:32] + low * send_buf[feat + 2 : feat + 3, cols]
        for k in range(STEPS):
            result = result + ret_recv[k, :, cols]
        out_ref[:, cols] = result


def per_device(n, points, values, inverse_scale):
    rhs, pts = values.shape
    vmem = pl.BlockSpec(memory_space=pltpu.VMEM)
    return pl.pallas_call(
        functools.partial(body, n),
        out_shape=jax.ShapeDtypeStruct((rhs, pts), f32),
        in_specs=[pl.BlockSpec(memory_space=pltpu.SMEM)] + [pl.BlockSpec(memory_space=pl.ANY)] * 2,
        out_specs=vmem,
        scratch_shapes=[
            pltpu.VMEM((32, pts), f32),
            pltpu.VMEM((STEPS, 32, pts), f32),
            pltpu.VMEM((pts, 128), bf16),
            pltpu.VMEM((3, 128, pts), bf16),
            pltpu.VMEM((3, 32, pts), bf16),
            pltpu.VMEM((3, 32, pts), f8),
            pltpu.VMEM((T, pts), f32),
            pltpu.VMEM((T, pts), bf16),
            pltpu.VMEM((T, pts), f8),
            pltpu.VMEM((T, pts), bf16),
            pltpu.VMEM((T, pts), f8),
            pltpu.VMEM((4, 32, pts), f32),
            pltpu.VMEM((4, 16, pts), f32),
            pltpu.VMEM((32, pts), f32),
            pltpu.VMEM((16, pts), f32),
            pltpu.VMEM((STEPS, rhs, pts), f32),
            pltpu.VMEM((STEPS, rhs, pts), f32),
            pltpu.VMEM(points.shape, f32),
            pltpu.VMEM(values.shape, f32),
            pltpu.SemaphoreType.DMA((STEPS,)),
            pltpu.SemaphoreType.DMA((STEPS,)),
            pltpu.SemaphoreType.DMA((STEPS,)),
            pltpu.SemaphoreType.DMA((STEPS,)),
            pltpu.SemaphoreType.DMA((2,)),
        ],
        compiler_params=pltpu.CompilerParams(
            collective_id=0, has_side_effects=True, vmem_limit_bytes=48 << 20
        ),
        name="matern",
    )(inverse_scale, points, values)


def solution(mesh):
    placed = (P(None, "blk"), P(None, "blk"), P())
    return jax.shard_map(
        functools.partial(per_device, mesh.shape["blk"]),
        mesh=mesh, in_specs=placed, out_specs=P(None, "blk"), check_vma=False,
    )
```

```python
import functools
import math

import jax
import jax.numpy as jnp
from jax import lax
from jax.experimental import pallas as pl
from jax.experimental.pallas import tpu as pltpu
from jax.sharding import PartitionSpec as P

STEPS = 4
LN2 = math.log(2.0)
SHIFT = 1.5 / LN2
BUMP = 0.75 / LN2**2
FACTOR = LN2**2 / 3.0
POINT_SCALE = math.sqrt(5.0) / LN2
UP = 14
V8_MAX = 240.0
MESH = pl.DeviceIdType.MESH

bf16, f32, f8 = jnp.bfloat16, jnp.float32, jnp.float8_e4m3fn
T = 256
OWN_SLOT, NO_SLOT = 2, 3


def dot(a, b, transposed=False):
    dims = (((1,), (1 if transposed else 0,)), ((), ()))
    return lax.dot_general(a, b, dims, preferred_element_type=f32)


def matern(s):
    s = jnp.maximum(s, 1e-30)
    t = s * lax.rsqrt(s)
    y = t + SHIFT
    return (y * y + BUMP) * jnp.exp2(UP - t)


def parts3(x):
    high = x.astype(bf16).astype(f32)
    rest = x - high
    middle = rest.astype(bf16).astype(f32)
    return high, middle, rest - middle


def body(
    n,
    scale_hbm, points_ref, values_ref, out_ref,
    send_buf, recv_buf, home_t, b_ref, v_ref, v8_ref,
    s_ref, kh0, kl0, kh1, kl1, oq, oq8, op, op8, ret_send, ret_recv,
    points_buf, values_buf, scale_ref, send_sem, recv_sem, rsend_sem, rrecv_sem, load_sem,
):
    me = lax.axis_index("blk")
    loads = [
        pltpu.make_async_copy(points_ref, points_buf, load_sem.at[0]),
        pltpu.make_async_copy(values_ref, values_buf, load_sem.at[1]),
        pltpu.make_async_copy(scale_hbm, scale_ref, load_sem.at[2]),
    ]
    for load in loads:
        load.start()
    feat, pts = points_ref.shape
    nc = pts // T
    own_steps = nc // 2 + 1
    total = own_steps + STEPS * nc
    first = own_steps
    high_refs, low_refs = (kh0, kh1), (kl0, kl1)

    def ahead(d):
        return lax.rem(me + n - d, n)

    def behind(d):
        return lax.rem(me + d, n)

    odd = 1 - lax.rem(me, 2)
    partner = me - 1 + 2 * odd
    barrier = pltpu.get_barrier_semaphore()
    for other in (ahead(2), partner):
        pl.semaphore_signal(barrier, inc=1, device_id=(other,), device_id_type=MESH)

    for load in loads:
        load.wait()
    norm = jnp.zeros((1, pts), f32)
    for r in range(feat):
        w = points_buf[r : r + 1, :] * (scale_ref[r] * POINT_SCALE)
        send_buf[r : r + 1, :] = w
        norm = norm + w * w
    scaled = values_buf[...] * (FACTOR * 2.0**-UP)
    largest = jnp.max(jnp.max(jnp.abs(scaled), axis=0, keepdims=True), axis=1, keepdims=True)
    send_buf[feat : feat + 1, :] = norm
    send_buf[feat + 1 : feat + 2, :] = jnp.ones((1, pts), f32)
    send_buf[feat + 2 : feat + 3, :] = jnp.broadcast_to(
        jnp.maximum(largest, 1e-30) * (1.0 / V8_MAX), (1, pts)
    )
    send_buf[feat + 3 : 16, :] = jnp.zeros((13 - feat, pts), f32)
    send_buf[16:32, :] = scaled


    def distance(k):
        even_order = jnp.where(k == 0, 1, jnp.where(k == 1, 3, jnp.where(k == 2, 4, 2)))
        odd_order = jnp.where(k == 0, 2, jnp.where(k == 1, 4, jnp.where(k == 2, 3, 1)))
        return jnp.where(odd == 1, odd_order, even_order)

    def block_copy(source, number, target, slot):
        return pltpu.make_async_remote_copy(
            src_ref=source,
            dst_ref=recv_buf.at[slot],
            send_sem=send_sem.at[number],
            recv_sem=recv_sem.at[slot],
            device_id=(target,),
            device_id_type=MESH,
        )

    def first_copy():
        return block_copy(send_buf, 0, behind(2), 3 - 3 * odd)

    def relay(source):
        block_copy(source, 1, behind(2), 2 - odd).start()
        block_copy(source, 2, partner, 3 - 2 * odd).start()

    def arrived(slot):
        block_copy(send_buf, 0, partner, slot).wait_recv()

    def return_copy(k):
        return pltpu.make_async_remote_copy(
            src_ref=ret_send.at[k],
            dst_ref=ret_recv.at[distance(k) - 1],
            send_sem=rsend_sem.at[k],
            recv_sem=rrecv_sem.at[distance(k) - 1],
            device_id=(ahead(distance(k)),),
            device_id_type=MESH,
        )

    pl.semaphore_wait(barrier, 2)

    @pl.when(odd == 1)
    def _():
        first_copy().start()
        block_copy(send_buf, 3, partner, 0).start()

    def prepare(source, slot):
        for c in range(nc):
            cols = slice(c * T, (c + 1) * T)
            high, middle, low = (q.astype(bf16) for q in parts3(source[0:16, cols]))
            for g, part in enumerate((high, middle, high, middle, low, high)):
                b_ref[slot, 16 * g : 16 * g + 16, cols] = part
            v = source[16:32, cols]
            vh = v.astype(bf16)
            v_ref[slot, 0:16, cols] = vh
            v_ref[slot, 16:32, cols] = (v - vh.astype(f32)).astype(bf16)
            v8 = v * (1.0 / source[feat + 2 : feat + 3, cols])
            v8_ref[slot, :, cols] = jnp.concatenate([v8, jnp.zeros_like(v8)], 0).astype(f8)

    row = lax.broadcasted_iota(jnp.int32, (16, T), 0)
    nothing = jnp.zeros((32, T), f32)
    for c in range(nc):
        cols = slice(c * T, (c + 1) * T)
        y = jnp.where(
            row < feat,
            -2.0 * send_buf[0:16, cols],
            jnp.where(row == feat, 1.0, jnp.where(row == feat + 1, send_buf[feat : feat + 1, cols], 0.0)),
        )
        high, middle, low = parts3(y)
        left = jnp.concatenate([high, high, middle, middle, high, low, nothing], 0)
        home_t[cols, :] = left.T.astype(bf16)
    for slot in range(3):
        b_ref[slot, 96:128, :] = jnp.zeros((32, pts), bf16)
    prepare(send_buf, OWN_SLOT)
    for ref in (op, op8, oq, oq8):
        ref[...] = jnp.zeros_like(ref)

    def place(g):
        v = g - first
        visit = jnp.logical_and(v >= 0, v < STEPS * nc)
        k = jnp.clip(v, 0, STEPS * nc - 1) // nc
        own = jnp.where(v < 0, g, g - STEPS * nc)
        slot = jnp.where(visit, lax.rem(k, 2), OWN_SLOT)
        offset = jnp.where(visit, jnp.clip(v, 0, STEPS * nc - 1) - k * nc, own)
        once = jnp.logical_or(own == 0, own == nc // 2)
        sums = jnp.where(visit, lax.rem(k, 2), jnp.where(once, NO_SLOT, OWN_SLOT))
        return slot, offset, sums

    def column(j, offset):
        return pl.ds(pl.multiple_of(lax.rem(j + offset, nc) * T, T), T)

    def cross(where, j):
        slot, offset, _ = where
        s_ref[:, j * T : (j + 1) * T] = dot(
            home_t[j * T : (j + 1) * T, :], b_ref[slot, :, column(j, offset)]
        )

    def elementwise(parity, j):
        for a in range(0, T, 32):
            rows, cols = slice(a, a + 32), slice(j * T, (j + 1) * T)
            k = matern(s_ref[rows, cols])
            high = k.astype(bf16)
            high_refs[parity][rows, cols] = high
            low_refs[parity][rows, cols] = (k - high.astype(f32)).astype(f8)

    def apply(where, parity, j):
        slot, offset, sums = where
        tile, cols = slice(j * T, (j + 1) * T), column(j, offset)
        kh, kl = high_refs[parity][:, tile], low_refs[parity][:, tile]
        op[:, tile] += dot(v_ref[slot, :, cols], kh, True)
        oq[sums, :, cols] += dot(v_ref[OWN_SLOT, :, tile], kh)
        op8[:, tile] += dot(v8_ref[slot, 0:16, cols], kl, True)
        oq8[sums, :, cols] += dot(v8_ref[OWN_SLOT, 0:16, tile], kl)

    def take(k):
        @pl.when(jnp.logical_or(odd == 1, k < 2))
        def _():
            arrived(k)

        @pl.when(jnp.logical_and(odd == 1, k == 0))
        def _():
            relay(recv_buf.at[0])

        prepare(recv_buf.at[k], lax.rem(k, 2))

    def settle(scale):
        op[0:16, :] += op8[...] * scale
        op8[...] = jnp.zeros_like(op8)

    def give_back(k):
        slot = lax.rem(k, 2)
        scale = send_buf[feat + 2 : feat + 3, :]
        ret_send[k] = oq[slot, 0:16, :] + oq[slot, 16:32, :] + oq8[slot] * scale
        return_copy(k).start()
        oq[slot] = jnp.zeros(oq.shape[1:], f32)
        oq8[slot] = jnp.zeros(oq8.shape[1:], f32)
        settle(recv_buf[k, feat + 2 : feat + 3, :])

    def events(g):
        @pl.when(jnp.logical_and(g == 2, odd == 0))
        def _():
            first_copy().start()

        due = g - first + 1

        @pl.when(jnp.logical_and(lax.rem(due, nc) == 0, jnp.logical_and(due >= 0, due < STEPS * nc)))
        def _():
            take(due // nc)

        @pl.when(jnp.logical_and(g == 10, odd == 0))
        def _():
            arrived(3)
            relay(recv_buf.at[3])

        @pl.when(jnp.logical_and(g == 18, odd == 0))
        def _():
            arrived(2)
            block_copy(recv_buf.at[2], 3, partner, 2).start()

        done = g - first - 1

        @pl.when(done == 0)
        def _():
            settle(send_buf[feat + 2 : feat + 3, :])

        @pl.when(jnp.logical_and(lax.rem(done, nc) == 0, done > 0))
        def _():
            give_back(done // nc - 1)

    def work(g, parity):
        before, after = place(g - 1), place(jnp.minimum(g + 1, total - 1))
        for j in range(nc):
            elementwise(parity, j)
            cross(after, j)
            apply(before, 1 - parity, j)

    start, second = place(jnp.int32(0)), place(jnp.int32(1))
    for j in range(nc):
        cross(start, j)
    for j in range(nc):
        elementwise(0, j)
        cross(second, j)
    def pair(h, carry):
        g = 2 * h + 1
        work(g, 1)
        events(g + 1)
        work(g + 1, 0)
        return carry

    lax.fori_loop(0, (total - 1) // 2, pair, 0)
    final = place(jnp.int32(total - 1))
    for j in range(nc):
        apply(final, 0, j)

    give_back(STEPS - 1)

    for k in range(STEPS):
        block_copy(send_buf, k, partner, 0).wait_send()
        return_copy(k).wait_send()
        return_copy(k).wait_recv()
    for c in range(nc):
        cols = slice(c * T, (c + 1) * T)
        low = op8[:, cols] + oq8[OWN_SLOT, :, cols]
        sums = op[:, cols] + oq[OWN_SLOT, :, cols]
        result = sums[0:16] + sums[16:32] + low * send_buf[feat + 2 : feat + 3, cols]
        for k in range(STEPS):
            result = result + ret_recv[k, :, cols]
        out_ref[:, cols] = result


def per_device(n, points, values, inverse_scale):
    rhs, pts = values.shape
    vmem = pl.BlockSpec(memory_space=pltpu.VMEM)
    return pl.pallas_call(
        functools.partial(body, n),
        out_shape=jax.ShapeDtypeStruct((rhs, pts), f32),
        in_specs=[pl.BlockSpec(memory_space=pltpu.HBM)] * 3,
        out_specs=vmem,
        scratch_shapes=[
            pltpu.VMEM((32, pts), f32),
            pltpu.VMEM((STEPS, 32, pts), f32),
            pltpu.VMEM((pts, 128), bf16),
            pltpu.VMEM((3, 128, pts), bf16),
            pltpu.VMEM((3, 32, pts), bf16),
            pltpu.VMEM((3, 32, pts), f8),
            pltpu.VMEM((T, pts), f32),
            pltpu.VMEM((T, pts), bf16),
            pltpu.VMEM((T, pts), f8),
            pltpu.VMEM((T, pts), bf16),
            pltpu.VMEM((T, pts), f8),
            pltpu.VMEM((4, 32, pts), f32),
            pltpu.VMEM((4, 16, pts), f32),
            pltpu.VMEM((32, pts), f32),
            pltpu.VMEM((16, pts), f32),
            pltpu.VMEM((STEPS, rhs, pts), f32),
            pltpu.VMEM((STEPS, rhs, pts), f32),
            pltpu.VMEM(points.shape, f32),
            pltpu.VMEM(values.shape, f32),
            pltpu.SMEM(inverse_scale.shape, f32),
            pltpu.SemaphoreType.DMA((STEPS,)),
            pltpu.SemaphoreType.DMA((STEPS,)),
            pltpu.SemaphoreType.DMA((STEPS,)),
            pltpu.SemaphoreType.DMA((STEPS,)),
            pltpu.SemaphoreType.DMA((3,)),
        ],
        compiler_params=pltpu.CompilerParams(
            collective_id=0, has_side_effects=True, vmem_limit_bytes=63 << 20
        ),
        name="matern",
    )(inverse_scale, points, values)


def solution(mesh):
    placed = (P(None, "blk"), P(None, "blk"), P())
    return jax.shard_map(
        functools.partial(per_device, mesh.shape["blk"]),
        mesh=mesh, in_specs=placed, out_specs=P(None, "blk"), check_vma=False,
    )
```

```python
import functools
import math

import jax
import jax.numpy as jnp
from jax import lax
from jax.experimental import pallas as pl
from jax.experimental.pallas import tpu as pltpu
from jax.sharding import PartitionSpec as P

STEPS = 4
LN2 = math.log(2.0)
SHIFT = 1.5 / LN2
BUMP = 0.75 / LN2**2
FACTOR = LN2**2 / 3.0
POINT_SCALE = math.sqrt(5.0) / LN2
UP = 14
V8_MAX = 240.0
MESH = pl.DeviceIdType.MESH

bf16, f32, f8 = jnp.bfloat16, jnp.float32, jnp.float8_e4m3fn
T = 256
OWN_SLOT, NO_SLOT = 2, 3


def dot(a, b, transposed=False):
    dims = (((1,), (1 if transposed else 0,)), ((), ()))
    return lax.dot_general(a, b, dims, preferred_element_type=f32)


def matern(s):
    s = jnp.maximum(s, 1e-30)
    t = s * lax.rsqrt(s)
    y = t + SHIFT
    return (y * y + BUMP) * jnp.exp2(UP - t)


def parts3(x):
    high = x.astype(bf16).astype(f32)
    rest = x - high
    middle = rest.astype(bf16).astype(f32)
    return high, middle, rest - middle


def body(
    n,
    scale_hbm, points_ref, values_ref, out_ref,
    send_buf, recv_buf, home_t, b_ref, v_ref, v8_ref,
    s_ref, kh0, kl0, kh1, kl1, oq, oq8, op, op8, ret_send, ret_recv,
    points_buf, values_buf, scale_ref, send_sem, recv_sem, rsend_sem, rrecv_sem, load_sem,
):
    me = lax.axis_index("blk")
    loads = [
        pltpu.make_async_copy(points_ref, points_buf, load_sem.at[0]),
        pltpu.make_async_copy(values_ref, values_buf, load_sem.at[1]),
        pltpu.make_async_copy(scale_hbm, scale_ref, load_sem.at[2]),
    ]
    for load in loads:
        load.start()
    feat, pts = points_ref.shape
    nc = pts // T
    own_steps = nc // 2 + 1
    total = own_steps + STEPS * nc
    first = own_steps
    high_refs, low_refs = (kh0, kh1), (kl0, kl1)

    def ahead(d):
        return lax.rem(me + n - d, n)

    def behind(d):
        return lax.rem(me + d, n)

    odd = 1 - lax.rem(me, 2)
    partner = me - 1 + 2 * odd
    barrier = pltpu.get_barrier_semaphore()
    for other in (ahead(2), partner):
        pl.semaphore_signal(barrier, inc=1, device_id=(other,), device_id_type=MESH)

    for load in loads:
        load.wait()
    norm = jnp.zeros((1, pts), f32)
    for r in range(feat):
        w = points_buf[r : r + 1, :] * (scale_ref[r] * POINT_SCALE)
        send_buf[r : r + 1, :] = w
        norm = norm + w * w
    scaled = values_buf[...] * (FACTOR * 2.0**-UP)
    largest = jnp.max(jnp.max(jnp.abs(scaled), axis=0, keepdims=True), axis=1, keepdims=True)
    send_buf[feat : feat + 1, :] = norm
    send_buf[feat + 1 : feat + 2, :] = jnp.ones((1, pts), f32)
    send_buf[feat + 2 : feat + 3, :] = jnp.broadcast_to(
        jnp.maximum(largest, 1e-30) * (1.0 / V8_MAX), (1, pts)
    )
    send_buf[feat + 3 : 16, :] = jnp.zeros((13 - feat, pts), f32)
    send_buf[16:32, :] = scaled


    def distance(k):
        even_order = jnp.where(k == 0, 1, jnp.where(k == 1, 3, jnp.where(k == 2, 4, 2)))
        odd_order = jnp.where(k == 0, 2, jnp.where(k == 1, 4, jnp.where(k == 2, 3, 1)))
        return jnp.where(odd == 1, odd_order, even_order)

    def block_copy(source, number, target, slot):
        return pltpu.make_async_remote_copy(
            src_ref=source,
            dst_ref=recv_buf.at[slot],
            send_sem=send_sem.at[number],
            recv_sem=recv_sem.at[slot],
            device_id=(target,),
            device_id_type=MESH,
        )

    def first_copy():
        return block_copy(send_buf, 0, behind(2), 3 - 3 * odd)

    def relay(source):
        block_copy(source, 1, behind(2), 2 - odd).start()
        block_copy(source, 2, partner, 3 - 2 * odd).start()

    def arrived(slot):
        block_copy(send_buf, 0, partner, slot).wait_recv()

    def return_copy(k):
        return pltpu.make_async_remote_copy(
            src_ref=ret_send.at[k],
            dst_ref=ret_recv.at[distance(k) - 1],
            send_sem=rsend_sem.at[k],
            recv_sem=rrecv_sem.at[distance(k) - 1],
            device_id=(ahead(distance(k)),),
            device_id_type=MESH,
        )

    pl.semaphore_wait(barrier, 2)

    @pl.when(odd == 1)
    def _():
        first_copy().start()
        block_copy(send_buf, 3, partner, 0).start()

    def prepare(source, slot):
        for c in range(nc):
            cols = slice(c * T, (c + 1) * T)
            high, middle, low = (q.astype(bf16) for q in parts3(source[0:16, cols]))
            for g, part in enumerate((high, middle, high, middle, low, high)):
                b_ref[slot, 16 * g : 16 * g + 16, cols] = part
            v = source[16:32, cols]
            vh = v.astype(bf16)
            v_ref[slot, 0:16, cols] = vh
            v_ref[slot, 16:32, cols] = (v - vh.astype(f32)).astype(bf16)
            v8 = v * (1.0 / source[feat + 2 : feat + 3, cols])
            v8_ref[slot, :, cols] = jnp.concatenate([v8, jnp.zeros_like(v8)], 0).astype(f8)

    row = lax.broadcasted_iota(jnp.int32, (16, T), 0)
    nothing = jnp.zeros((32, T), f32)
    for c in range(nc):
        cols = slice(c * T, (c + 1) * T)
        y = jnp.where(
            row < feat,
            -2.0 * send_buf[0:16, cols],
            jnp.where(row == feat, 1.0, jnp.where(row == feat + 1, send_buf[feat : feat + 1, cols], 0.0)),
        )
        high, middle, low = parts3(y)
        left = jnp.concatenate([high, high, middle, middle, high, low, nothing], 0)
        home_t[cols, :] = left.T.astype(bf16)
    for slot in range(3):
        b_ref[slot, 96:128, :] = jnp.zeros((32, pts), bf16)
    prepare(send_buf, OWN_SLOT)
    for ref in (op, op8, oq, oq8):
        ref[...] = jnp.zeros_like(ref)

    def place(g):
        v = g - first
        visit = jnp.logical_and(v >= 0, v < STEPS * nc)
        k = jnp.clip(v, 0, STEPS * nc - 1) // nc
        own = jnp.where(v < 0, g, g - STEPS * nc)
        slot = jnp.where(visit, lax.rem(k, 2), OWN_SLOT)
        offset = jnp.where(visit, jnp.clip(v, 0, STEPS * nc - 1) - k * nc, own)
        once = jnp.logical_or(own == 0, own == nc // 2)
        sums = jnp.where(visit, lax.rem(k, 2), jnp.where(once, NO_SLOT, OWN_SLOT))
        return slot, offset, sums

    def column(j, offset):
        return pl.ds(pl.multiple_of(lax.rem(j + offset, nc) * T, T), T)

    def cross(where, j):
        slot, offset, _ = where
        s_ref[:, j * T : (j + 1) * T] = dot(
            home_t[j * T : (j + 1) * T, :], b_ref[slot, :, column(j, offset)]
        )

    def elementwise(parity, j):
        for a in range(0, T, 32):
            rows, cols = slice(a, a + 32), slice(j * T, (j + 1) * T)
            k = matern(s_ref[rows, cols])
            high = k.astype(bf16)
            high_refs[parity][rows, cols] = high
            low_refs[parity][rows, cols] = (k - high.astype(f32)).astype(f8)

    def apply(where, parity, j):
        slot, offset, sums = where
        tile, cols = slice(j * T, (j + 1) * T), column(j, offset)
        kh, kl = high_refs[parity][:, tile], low_refs[parity][:, tile]
        op[:, tile] += dot(v_ref[slot, :, cols], kh, True)
        oq[sums, :, cols] += dot(v_ref[OWN_SLOT, :, tile], kh)
        op8[:, tile] += dot(v8_ref[slot, 0:16, cols], kl, True)
        oq8[sums, :, cols] += dot(v8_ref[OWN_SLOT, 0:16, tile], kl)

    def take(k):
        @pl.when(jnp.logical_or(odd == 1, k < 2))
        def _():
            arrived(k)

        @pl.when(jnp.logical_and(odd == 1, k == 0))
        def _():
            relay(recv_buf.at[0])

        prepare(recv_buf.at[k], lax.rem(k, 2))

    def settle(scale):
        op[0:16, :] += op8[...] * scale
        op8[...] = jnp.zeros_like(op8)

    def give_back(k):
        slot = lax.rem(k, 2)
        scale = send_buf[feat + 2 : feat + 3, :]
        ret_send[k] = oq[slot, 0:16, :] + oq[slot, 16:32, :] + oq8[slot] * scale
        return_copy(k).start()
        oq[slot] = jnp.zeros(oq.shape[1:], f32)
        oq8[slot] = jnp.zeros(oq8.shape[1:], f32)
        settle(recv_buf[k, feat + 2 : feat + 3, :])

    def events(g):
        @pl.when(jnp.logical_and(g == 2, odd == 0))
        def _():
            first_copy().start()

        due = g - first + 1

        @pl.when(jnp.logical_and(lax.rem(due, nc) == 0, jnp.logical_and(due >= 0, due < STEPS * nc)))
        def _():
            take(due // nc)

        @pl.when(jnp.logical_and(g == 6, odd == 0))
        def _():
            arrived(3)
            relay(recv_buf.at[3])

        @pl.when(jnp.logical_and(g == 14, odd == 0))
        def _():
            arrived(2)
            block_copy(recv_buf.at[2], 3, partner, 2).start()

        done = g - first - 1

        @pl.when(done == 0)
        def _():
            settle(send_buf[feat + 2 : feat + 3, :])

        @pl.when(jnp.logical_and(lax.rem(done, nc) == 0, done > 0))
        def _():
            give_back(done // nc - 1)

    def work(g, parity):
        before, after = place(g - 1), place(jnp.minimum(g + 1, total - 1))
        for j in range(nc):
            elementwise(parity, j)
            cross(after, j)
            apply(before, 1 - parity, j)

    start, second = place(jnp.int32(0)), place(jnp.int32(1))
    for j in range(nc):
        cross(start, j)
    for j in range(nc):
        elementwise(0, j)
        cross(second, j)
    def pair(h, carry):
        g = 2 * h + 1
        work(g, 1)
        events(g + 1)
        work(g + 1, 0)
        return carry

    lax.fori_loop(0, (total - 1) // 2, pair, 0)
    final = place(jnp.int32(total - 1))
    for j in range(nc):
        apply(final, 0, j)

    give_back(STEPS - 1)

    for k in range(STEPS):
        block_copy(send_buf, k, partner, 0).wait_send()
        return_copy(k).wait_send()
        return_copy(k).wait_recv()
    for c in range(nc):
        cols = slice(c * T, (c + 1) * T)
        low = op8[:, cols] + oq8[OWN_SLOT, :, cols]
        sums = op[:, cols] + oq[OWN_SLOT, :, cols]
        result = sums[0:16] + sums[16:32] + low * send_buf[feat + 2 : feat + 3, cols]
        for k in range(STEPS):
            result = result + ret_recv[k, :, cols]
        out_ref[:, cols] = result


def per_device(n, points, values, inverse_scale):
    rhs, pts = values.shape
    vmem = pl.BlockSpec(memory_space=pltpu.VMEM)
    return pl.pallas_call(
        functools.partial(body, n),
        out_shape=jax.ShapeDtypeStruct((rhs, pts), f32),
        in_specs=[pl.BlockSpec(memory_space=pltpu.HBM)] * 3,
        out_specs=vmem,
        scratch_shapes=[
            pltpu.VMEM((32, pts), f32),
            pltpu.VMEM((STEPS, 32, pts), f32),
            pltpu.VMEM((pts, 128), bf16),
            pltpu.VMEM((3, 128, pts), bf16),
            pltpu.VMEM((3, 32, pts), bf16),
            pltpu.VMEM((3, 32, pts), f8),
            pltpu.VMEM((T, pts), f32),
            pltpu.VMEM((T, pts), bf16),
            pltpu.VMEM((T, pts), f8),
            pltpu.VMEM((T, pts), bf16),
            pltpu.VMEM((T, pts), f8),
            pltpu.VMEM((4, 32, pts), f32),
            pltpu.VMEM((4, 16, pts), f32),
            pltpu.VMEM((32, pts), f32),
            pltpu.VMEM((16, pts), f32),
            pltpu.VMEM((STEPS, rhs, pts), f32),
            pltpu.VMEM((STEPS, rhs, pts), f32),
            pltpu.VMEM(points.shape, f32),
            pltpu.VMEM(values.shape, f32),
            pltpu.SMEM(inverse_scale.shape, f32),
            pltpu.SemaphoreType.DMA((STEPS,)),
            pltpu.SemaphoreType.DMA((STEPS,)),
            pltpu.SemaphoreType.DMA((STEPS,)),
            pltpu.SemaphoreType.DMA((STEPS,)),
            pltpu.SemaphoreType.DMA((3,)),
        ],
        compiler_params=pltpu.CompilerParams(
            collective_id=0, has_side_effects=True, vmem_limit_bytes=63 << 20
        ),
        name="matern",
    )(inverse_scale, points, values)


def solution(mesh):
    placed = (P(None, "blk"), P(None, "blk"), P())
    return jax.shard_map(
        functools.partial(per_device, mesh.shape["blk"]),
        mesh=mesh, in_specs=placed, out_specs=P(None, "blk"), check_vma=False,
    )
```

```python
import functools
import math

import jax
import jax.numpy as jnp
from jax import lax
from jax.experimental import pallas as pl
from jax.experimental.pallas import tpu as pltpu
from jax.sharding import PartitionSpec as P

STEPS = 4
LN2 = math.log(2.0)
SHIFT = 1.5 / LN2
BUMP = 0.75 / LN2**2
FACTOR = LN2**2 / 3.0
POINT_SCALE = math.sqrt(5.0) / LN2
UP = 14
V8_MAX = 240.0
MESH = pl.DeviceIdType.MESH

bf16, f32, f8 = jnp.bfloat16, jnp.float32, jnp.float8_e4m3fn
T = 256
OWN_SLOT, NO_SLOT = 2, 3


def dot(a, b, transposed=False):
    dims = (((1,), (1 if transposed else 0,)), ((), ()))
    return lax.dot_general(a, b, dims, preferred_element_type=f32)


def matern(s):
    s = jnp.maximum(s, 1e-30)
    t = s * lax.rsqrt(s)
    y = t + SHIFT
    return (y * y + BUMP) * jnp.exp2(UP - t)


def parts3(x):
    high = x.astype(bf16).astype(f32)
    rest = x - high
    middle = rest.astype(bf16).astype(f32)
    return high, middle, rest - middle


def body(
    n,
    scale_hbm, points_ref, values_ref, out_ref,
    send_buf, recv_buf, home_t, b_ref, v_ref, v8_ref,
    s_ref, kh0, kl0, kh1, kl1, oq, oq8, op, op8, ret_send, ret_recv,
    points_buf, values_buf, scale_ref, send_sem, recv_sem, rsend_sem, rrecv_sem, load_sem,
):
    me = lax.axis_index("blk")
    loads = [
        pltpu.make_async_copy(points_ref, points_buf, load_sem.at[0]),
        pltpu.make_async_copy(values_ref, values_buf, load_sem.at[1]),
        pltpu.make_async_copy(scale_hbm, scale_ref, load_sem.at[2]),
    ]
    for load in loads:
        load.start()
    feat, pts = points_ref.shape
    nc = pts // T
    own_steps = nc // 2 + 1
    total = own_steps + STEPS * nc
    first = own_steps - 2
    high_refs, low_refs = (kh0, kh1), (kl0, kl1)

    def ahead(d):
        return lax.rem(me + n - d, n)

    def behind(d):
        return lax.rem(me + d, n)

    odd = 1 - lax.rem(me, 2)
    partner = me - 1 + 2 * odd
    barrier = pltpu.get_barrier_semaphore()
    for other in (ahead(2), partner):
        pl.semaphore_signal(barrier, inc=1, device_id=(other,), device_id_type=MESH)

    for load in loads:
        load.wait()
    norm = jnp.zeros((1, pts), f32)
    for r in range(feat):
        w = points_buf[r : r + 1, :] * (scale_ref[r] * POINT_SCALE)
        send_buf[r : r + 1, :] = w
        norm = norm + w * w
    scaled = values_buf[...] * (FACTOR * 2.0**-UP)
    largest = jnp.max(jnp.max(jnp.abs(scaled), axis=0, keepdims=True), axis=1, keepdims=True)
    send_buf[feat : feat + 1, :] = norm
    send_buf[feat + 1 : feat + 2, :] = jnp.ones((1, pts), f32)
    send_buf[feat + 2 : feat + 3, :] = jnp.broadcast_to(
        jnp.maximum(largest, 1e-30) * (1.0 / V8_MAX), (1, pts)
    )
    send_buf[feat + 3 : 16, :] = jnp.zeros((13 - feat, pts), f32)
    send_buf[16:32, :] = scaled


    def distance(k):
        even_order = jnp.where(k == 0, 1, jnp.where(k == 1, 3, jnp.where(k == 2, 4, 2)))
        odd_order = jnp.where(k == 0, 2, jnp.where(k == 1, 4, jnp.where(k == 2, 3, 1)))
        return jnp.where(odd == 1, odd_order, even_order)

    def block_copy(source, number, target, slot):
        return pltpu.make_async_remote_copy(
            src_ref=source,
            dst_ref=recv_buf.at[slot],
            send_sem=send_sem.at[number],
            recv_sem=recv_sem.at[slot],
            device_id=(target,),
            device_id_type=MESH,
        )

    def first_copy():
        return block_copy(send_buf, 0, behind(2), 3 - 3 * odd)

    def relay(source):
        block_copy(source, 1, behind(2), 2 - odd).start()
        block_copy(source, 2, partner, 3 - 2 * odd).start()

    def arrived(slot):
        block_copy(send_buf, 0, partner, slot).wait_recv()

    def return_copy(k):
        return pltpu.make_async_remote_copy(
            src_ref=ret_send.at[k],
            dst_ref=ret_recv.at[distance(k) - 1],
            send_sem=rsend_sem.at[k],
            recv_sem=rrecv_sem.at[distance(k) - 1],
            device_id=(ahead(distance(k)),),
            device_id_type=MESH,
        )

    pl.semaphore_wait(barrier, 2)

    @pl.when(odd == 1)
    def _():
        first_copy().start()
        block_copy(send_buf, 3, partner, 0).start()

    def prepare(source, slot):
        for c in range(nc):
            cols = slice(c * T, (c + 1) * T)
            high, middle, low = (q.astype(bf16) for q in parts3(source[0:16, cols]))
            for g, part in enumerate((high, middle, high, middle, low, high)):
                b_ref[slot, 16 * g : 16 * g + 16, cols] = part
            v = source[16:32, cols]
            vh = v.astype(bf16)
            v_ref[slot, 0:16, cols] = vh
            v_ref[slot, 16:32, cols] = (v - vh.astype(f32)).astype(bf16)
            v8 = v * (1.0 / source[feat + 2 : feat + 3, cols])
            v8_ref[slot, :, cols] = jnp.concatenate([v8, jnp.zeros_like(v8)], 0).astype(f8)

    row = lax.broadcasted_iota(jnp.int32, (16, T), 0)
    nothing = jnp.zeros((32, T), f32)
    for c in range(nc):
        cols = slice(c * T, (c + 1) * T)
        y = jnp.where(
            row < feat,
            -2.0 * send_buf[0:16, cols],
            jnp.where(row == feat, 1.0, jnp.where(row == feat + 1, send_buf[feat : feat + 1, cols], 0.0)),
        )
        high, middle, low = parts3(y)
        left = jnp.concatenate([high, high, middle, middle, high, low, nothing], 0)
        home_t[cols, :] = left.T.astype(bf16)
    for slot in range(3):
        b_ref[slot, 96:128, :] = jnp.zeros((32, pts), bf16)
    prepare(send_buf, OWN_SLOT)
    for ref in (op, op8, oq, oq8):
        ref[...] = jnp.zeros_like(ref)

    def place(g):
        v = g - first
        visit = jnp.logical_and(v >= 0, v < STEPS * nc)
        k = jnp.clip(v, 0, STEPS * nc - 1) // nc
        own = jnp.where(v < 0, g, g - STEPS * nc)
        slot = jnp.where(visit, lax.rem(k, 2), OWN_SLOT)
        offset = jnp.where(visit, jnp.clip(v, 0, STEPS * nc - 1) - k * nc, own)
        once = jnp.logical_or(own == 0, own == nc // 2)
        sums = jnp.where(visit, lax.rem(k, 2), jnp.where(once, NO_SLOT, OWN_SLOT))
        return slot, offset, sums

    def column(j, offset):
        return pl.ds(pl.multiple_of(lax.rem(j + offset, nc) * T, T), T)

    def cross(where, j):
        slot, offset, _ = where
        s_ref[:, j * T : (j + 1) * T] = dot(
            home_t[j * T : (j + 1) * T, :], b_ref[slot, :, column(j, offset)]
        )

    def elementwise(parity, j):
        for a in range(0, T, 32):
            rows, cols = slice(a, a + 32), slice(j * T, (j + 1) * T)
            k = matern(s_ref[rows, cols])
            high = k.astype(bf16)
            high_refs[parity][rows, cols] = high
            low_refs[parity][rows, cols] = (k - high.astype(f32)).astype(f8)

    def apply(where, parity, j):
        slot, offset, sums = where
        tile, cols = slice(j * T, (j + 1) * T), column(j, offset)
        kh, kl = high_refs[parity][:, tile], low_refs[parity][:, tile]
        op[:, tile] += dot(v_ref[slot, :, cols], kh, True)
        oq[sums, :, cols] += dot(v_ref[OWN_SLOT, :, tile], kh)
        op8[:, tile] += dot(v8_ref[slot, 0:16, cols], kl, True)
        oq8[sums, :, cols] += dot(v8_ref[OWN_SLOT, 0:16, tile], kl)

    def take(k):
        @pl.when(jnp.logical_or(odd == 1, k < 2))
        def _():
            arrived(k)

        @pl.when(jnp.logical_and(odd == 1, k == 0))
        def _():
            relay(recv_buf.at[0])

        prepare(recv_buf.at[k], lax.rem(k, 2))

    def settle(scale):
        op[0:16, :] += op8[...] * scale
        op8[...] = jnp.zeros_like(op8)

    def give_back(k):
        slot = lax.rem(k, 2)
        scale = send_buf[feat + 2 : feat + 3, :]
        ret_send[k] = oq[slot, 0:16, :] + oq[slot, 16:32, :] + oq8[slot] * scale
        return_copy(k).start()
        oq[slot] = jnp.zeros(oq.shape[1:], f32)
        oq8[slot] = jnp.zeros(oq8.shape[1:], f32)
        settle(recv_buf[k, feat + 2 : feat + 3, :])

    def events(g):
        @pl.when(jnp.logical_and(g == 2, odd == 0))
        def _():
            first_copy().start()

        due = g - first + 1

        @pl.when(jnp.logical_and(lax.rem(due, nc) == 0, jnp.logical_and(due >= 0, due < STEPS * nc)))
        def _():
            take(due // nc)

        @pl.when(jnp.logical_and(g == 6, odd == 0))
        def _():
            arrived(3)
            relay(recv_buf.at[3])

        @pl.when(jnp.logical_and(g == 14, odd == 0))
        def _():
            arrived(2)
            block_copy(recv_buf.at[2], 3, partner, 2).start()

        done = g - first - 1

        @pl.when(done == 0)
        def _():
            settle(send_buf[feat + 2 : feat + 3, :])

        @pl.when(jnp.logical_and(lax.rem(done, nc) == 0, done > 0))
        def _():
            give_back(done // nc - 1)

    def work(g, parity):
        before, after = place(g - 1), place(jnp.minimum(g + 1, total - 1))
        for j in range(nc):
            elementwise(parity, j)
            cross(after, j)
            apply(before, 1 - parity, j)

    start, second = place(jnp.int32(0)), place(jnp.int32(1))
    for j in range(nc):
        cross(start, j)
    for j in range(nc):
        elementwise(0, j)
        cross(second, j)
    def pair(h, carry):
        g = 2 * h + 1
        work(g, 1)
        events(g + 1)
        work(g + 1, 0)
        return carry

    lax.fori_loop(0, (total - 1) // 2, pair, 0)
    final = place(jnp.int32(total - 1))
    for j in range(nc):
        apply(final, 0, j)

    for k in range(STEPS):
        block_copy(send_buf, k, partner, 0).wait_send()
        return_copy(k).wait_send()
        return_copy(k).wait_recv()
    for c in range(nc):
        cols = slice(c * T, (c + 1) * T)
        low = op8[:, cols] + oq8[OWN_SLOT, :, cols]
        sums = op[:, cols] + oq[OWN_SLOT, :, cols]
        result = sums[0:16] + sums[16:32] + low * send_buf[feat + 2 : feat + 3, cols]
        for k in range(STEPS):
            result = result + ret_recv[k, :, cols]
        out_ref[:, cols] = result


def per_device(n, points, values, inverse_scale):
    rhs, pts = values.shape
    vmem = pl.BlockSpec(memory_space=pltpu.VMEM)
    return pl.pallas_call(
        functools.partial(body, n),
        out_shape=jax.ShapeDtypeStruct((rhs, pts), f32),
        in_specs=[pl.BlockSpec(memory_space=pltpu.HBM)] * 3,
        out_specs=vmem,
        scratch_shapes=[
            pltpu.VMEM((32, pts), f32),
            pltpu.VMEM((STEPS, 32, pts), f32),
            pltpu.VMEM((pts, 128), bf16),
            pltpu.VMEM((3, 128, pts), bf16),
            pltpu.VMEM((3, 32, pts), bf16),
            pltpu.VMEM((3, 32, pts), f8),
            pltpu.VMEM((T, pts), f32),
            pltpu.VMEM((T, pts), bf16),
            pltpu.VMEM((T, pts), f8),
            pltpu.VMEM((T, pts), bf16),
            pltpu.VMEM((T, pts), f8),
            pltpu.VMEM((4, 32, pts), f32),
            pltpu.VMEM((4, 16, pts), f32),
            pltpu.VMEM((32, pts), f32),
            pltpu.VMEM((16, pts), f32),
            pltpu.VMEM((STEPS, rhs, pts), f32),
            pltpu.VMEM((STEPS, rhs, pts), f32),
            pltpu.VMEM(points.shape, f32),
            pltpu.VMEM(values.shape, f32),
            pltpu.SMEM(inverse_scale.shape, f32),
            pltpu.SemaphoreType.DMA((STEPS,)),
            pltpu.SemaphoreType.DMA((STEPS,)),
            pltpu.SemaphoreType.DMA((STEPS,)),
            pltpu.SemaphoreType.DMA((STEPS,)),
            pltpu.SemaphoreType.DMA((3,)),
        ],
        compiler_params=pltpu.CompilerParams(
            collective_id=0, has_side_effects=True, vmem_limit_bytes=63 << 20
        ),
        name="matern",
    )(inverse_scale, points, values)


def solution(mesh):
    placed = (P(None, "blk"), P(None, "blk"), P())
    return jax.shard_map(
        functools.partial(per_device, mesh.shape["blk"]),
        mesh=mesh, in_specs=placed, out_specs=P(None, "blk"), check_vma=False,
    )
```

```python
import functools
import math

import jax
import jax.numpy as jnp
from jax import lax
from jax.experimental import pallas as pl
from jax.experimental.pallas import tpu as pltpu
from jax.sharding import PartitionSpec as P

STEPS = 4
LN2 = math.log(2.0)
SHIFT = 1.5 / LN2
BUMP = 0.75 / LN2**2
FACTOR = LN2**2 / 3.0
POINT_SCALE = math.sqrt(5.0) / LN2
UP = 14
V8_MAX = 240.0
MESH = pl.DeviceIdType.MESH

bf16, f32, f8 = jnp.bfloat16, jnp.float32, jnp.float8_e4m3fn
T = 256
OWN_SLOT, NO_SLOT = 2, 3


def dot(a, b, transposed=False):
    dims = (((1,), (1 if transposed else 0,)), ((), ()))
    return lax.dot_general(a, b, dims, preferred_element_type=f32)


def matern(s):
    s = jnp.maximum(s, 1e-30)
    t = s * lax.rsqrt(s)
    y = t + SHIFT
    return (y * y + BUMP) * jnp.exp2(UP - t)


def parts3(x):
    high = x.astype(bf16).astype(f32)
    rest = x - high
    middle = rest.astype(bf16).astype(f32)
    return high, middle, rest - middle


def body(
    n,
    scale_ref, points_ref, values_ref, out_ref,
    send_buf, recv_buf, home_t, b_ref, v_ref, v8_ref,
    s_ref, kh0, kl0, kh1, kl1, oq, oq8, op, op8, ret_send, ret_recv,
    points_buf, values_buf, send_sem, recv_sem, rsend_sem, rrecv_sem, load_sem,
):
    me = lax.axis_index("blk")
    loads = [
        pltpu.make_async_copy(points_ref, points_buf, load_sem.at[0]),
        pltpu.make_async_copy(values_ref, values_buf, load_sem.at[1]),
    ]
    for load in loads:
        load.start()
    feat, pts = points_ref.shape
    nc = pts // T
    own_steps = nc // 2 + 1
    total = own_steps + STEPS * nc
    first = own_steps
    high_refs, low_refs = (kh0, kh1), (kl0, kl1)

    def ahead(d):
        return lax.rem(me + n - d, n)

    def behind(d):
        return lax.rem(me + d, n)

    odd = 1 - lax.rem(me, 2)
    partner = me - 1 + 2 * odd
    barrier = pltpu.get_barrier_semaphore()
    for other in (ahead(2), partner):
        pl.semaphore_signal(barrier, inc=1, device_id=(other,), device_id_type=MESH)

    for load in loads:
        load.wait()
    norm = jnp.zeros((1, pts), f32)
    for r in range(feat):
        w = points_buf[r : r + 1, :] * (scale_ref[r] * POINT_SCALE)
        send_buf[r : r + 1, :] = w
        norm = norm + w * w
    scaled = values_buf[...] * (FACTOR * 2.0**-UP)
    largest = jnp.max(jnp.max(jnp.abs(scaled), axis=0, keepdims=True), axis=1, keepdims=True)
    send_buf[feat : feat + 1, :] = norm
    send_buf[feat + 1 : feat + 2, :] = jnp.ones((1, pts), f32)
    send_buf[feat + 2 : feat + 3, :] = jnp.broadcast_to(
        jnp.maximum(largest, 1e-30) * (1.0 / V8_MAX), (1, pts)
    )
    send_buf[feat + 3 : 16, :] = jnp.zeros((13 - feat, pts), f32)
    send_buf[16:32, :] = scaled


    def distance(k):
        even_order = jnp.where(k == 0, 1, jnp.where(k == 1, 3, jnp.where(k == 2, 4, 2)))
        odd_order = jnp.where(k == 0, 2, jnp.where(k == 1, 4, jnp.where(k == 2, 3, 1)))
        return jnp.where(odd == 1, odd_order, even_order)

    def block_copy(source, number, target, slot):
        return pltpu.make_async_remote_copy(
            src_ref=source,
            dst_ref=recv_buf.at[slot],
            send_sem=send_sem.at[number],
            recv_sem=recv_sem.at[slot],
            device_id=(target,),
            device_id_type=MESH,
        )

    def first_copy():
        return block_copy(send_buf, 0, behind(2), 3 - 3 * odd)

    def relay(source):
        block_copy(source, 1, behind(2), 2 - odd).start()
        block_copy(source, 2, partner, 3 - 2 * odd).start()

    def arrived(slot):
        block_copy(send_buf, 0, partner, slot).wait_recv()

    def return_copy(k):
        return pltpu.make_async_remote_copy(
            src_ref=ret_send.at[k],
            dst_ref=ret_recv.at[distance(k) - 1],
            send_sem=rsend_sem.at[k],
            recv_sem=rrecv_sem.at[distance(k) - 1],
            device_id=(ahead(distance(k)),),
            device_id_type=MESH,
        )

    pl.semaphore_wait(barrier, 2)

    @pl.when(odd == 1)
    def _():
        first_copy().start()
        block_copy(send_buf, 3, partner, 0).start()

    def prepare(source, slot):
        for c in range(nc):
            cols = slice(c * T, (c + 1) * T)
            high, middle, low = (q.astype(bf16) for q in parts3(source[0:16, cols]))
            for g, part in enumerate((high, middle, high, middle, low, high)):
                b_ref[slot, 16 * g : 16 * g + 16, cols] = part
            v = source[16:32, cols]
            vh = v.astype(bf16)
            v_ref[slot, 0:16, cols] = vh
            v_ref[slot, 16:32, cols] = (v - vh.astype(f32)).astype(bf16)
            v8 = v * (1.0 / source[feat + 2 : feat + 3, cols])
            v8_ref[slot, :, cols] = jnp.concatenate([v8, jnp.zeros_like(v8)], 0).astype(f8)

    row = lax.broadcasted_iota(jnp.int32, (16, T), 0)
    nothing = jnp.zeros((32, T), f32)
    for c in range(nc):
        cols = slice(c * T, (c + 1) * T)
        y = jnp.where(
            row < feat,
            -2.0 * send_buf[0:16, cols],
            jnp.where(row == feat, 1.0, jnp.where(row == feat + 1, send_buf[feat : feat + 1, cols], 0.0)),
        )
        high, middle, low = parts3(y)
        left = jnp.concatenate([high, high, middle, middle, high, low, nothing], 0)
        home_t[cols, :] = left.T.astype(bf16)
    for slot in range(3):
        b_ref[slot, 96:128, :] = jnp.zeros((32, pts), bf16)
    prepare(send_buf, OWN_SLOT)
    for ref in (op, op8, oq, oq8):
        ref[...] = jnp.zeros_like(ref)

    def place(g):
        v = g - first
        visit = jnp.logical_and(v >= 0, v < STEPS * nc)
        k = jnp.clip(v, 0, STEPS * nc - 1) // nc
        own = jnp.where(v < 0, g, g - STEPS * nc)
        slot = jnp.where(visit, lax.rem(k, 2), OWN_SLOT)
        offset = jnp.where(visit, jnp.clip(v, 0, STEPS * nc - 1) - k * nc, own)
        once = jnp.logical_or(own == 0, own == nc // 2)
        sums = jnp.where(visit, lax.rem(k, 2), jnp.where(once, NO_SLOT, OWN_SLOT))
        return slot, offset, sums

    def column(j, offset):
        return pl.ds(pl.multiple_of(lax.rem(j + offset, nc) * T, T), T)

    def cross(where, j):
        slot, offset, _ = where
        s_ref[:, j * T : (j + 1) * T] = dot(
            home_t[j * T : (j + 1) * T, :], b_ref[slot, :, column(j, offset)]
        )

    def elementwise(parity, j):
        for a in range(0, T, 32):
            rows, cols = slice(a, a + 32), slice(j * T, (j + 1) * T)
            k = matern(s_ref[rows, cols])
            high = k.astype(bf16)
            high_refs[parity][rows, cols] = high
            low_refs[parity][rows, cols] = (k - high.astype(f32)).astype(f8)

    def apply(where, parity, j):
        slot, offset, sums = where
        tile, cols = slice(j * T, (j + 1) * T), column(j, offset)
        kh, kl = high_refs[parity][:, tile], low_refs[parity][:, tile]
        op[:, tile] += dot(v_ref[slot, :, cols], kh, True)
        oq[sums, :, cols] += dot(v_ref[OWN_SLOT, :, tile], kh)
        op8[:, tile] += dot(v8_ref[slot, 0:16, cols], kl, True)
        oq8[sums, :, cols] += dot(v8_ref[OWN_SLOT, 0:16, tile], kl)

    def take(k):
        @pl.when(jnp.logical_or(odd == 1, k < 2))
        def _():
            arrived(k)

        @pl.when(jnp.logical_and(odd == 1, k == 0))
        def _():
            relay(recv_buf.at[0])

        prepare(recv_buf.at[k], lax.rem(k, 2))

    def settle(scale):
        op[0:16, :] += op8[...] * scale
        op8[...] = jnp.zeros_like(op8)

    def give_back(k):
        slot = lax.rem(k, 2)
        scale = send_buf[feat + 2 : feat + 3, :]
        ret_send[k] = oq[slot, 0:16, :] + oq[slot, 16:32, :] + oq8[slot] * scale
        return_copy(k).start()
        oq[slot] = jnp.zeros(oq.shape[1:], f32)
        oq8[slot] = jnp.zeros(oq8.shape[1:], f32)
        settle(recv_buf[k, feat + 2 : feat + 3, :])

    def events(g):
        @pl.when(jnp.logical_and(g == 2, odd == 0))
        def _():
            first_copy().start()

        due = g - first + 1

        @pl.when(jnp.logical_and(lax.rem(due, nc) == 0, jnp.logical_and(due >= 0, due < STEPS * nc)))
        def _():
            take(due // nc)

        @pl.when(jnp.logical_and(g == 6, odd == 0))
        def _():
            arrived(3)
            relay(recv_buf.at[3])

        @pl.when(jnp.logical_and(g == 14, odd == 0))
        def _():
            arrived(2)
            block_copy(recv_buf.at[2], 3, partner, 2).start()

        done = g - first - 1

        @pl.when(done == 0)
        def _():
            settle(send_buf[feat + 2 : feat + 3, :])

        @pl.when(jnp.logical_and(lax.rem(done, nc) == 0, done > 0))
        def _():
            give_back(done // nc - 1)

    def work(g, parity):
        before, after = place(g - 1), place(jnp.minimum(g + 1, total - 1))
        for j in range(nc):
            elementwise(parity, j)
            cross(after, j)
            apply(before, 1 - parity, j)

    start, second = place(jnp.int32(0)), place(jnp.int32(1))
    for j in range(nc):
        cross(start, j)
    for j in range(nc):
        elementwise(0, j)
        cross(second, j)
    def pair(h, carry):
        g = 2 * h + 1
        work(g, 1)
        events(g + 1)
        work(g + 1, 0)
        return carry

    lax.fori_loop(0, (total - 1) // 2, pair, 0)
    slot, offset, _ = place(jnp.int32(total - 1))
    last, last_slot = STEPS - 1, (STEPS - 1) % 2
    for j in range(nc):
        tile, cols = slice(j * T, (j + 1) * T), column(j, offset)
        oq[last_slot, :, cols] += dot(v_ref[OWN_SLOT, :, tile], kh0[:, tile])
        oq8[last_slot, :, cols] += dot(v8_ref[OWN_SLOT, 0:16, tile], kl0[:, tile])
    ret_send[last] = (
        oq[last_slot, 0:16, :] + oq[last_slot, 16:32, :] + oq8[last_slot] * send_buf[feat + 2 : feat + 3, :]
    )
    return_copy(last).start()
    for j in range(nc):
        tile, cols = slice(j * T, (j + 1) * T), column(j, offset)
        op[:, tile] += dot(v_ref[slot, :, cols], kh0[:, tile], True)
        op8[:, tile] += dot(v8_ref[slot, 0:16, cols], kl0[:, tile], True)
    for c in range(nc):
        cols = slice(c * T, (c + 1) * T)
        sums = op[:, cols] + oq[OWN_SLOT, :, cols]
        low = op8[:, cols] * recv_buf[last, feat + 2 : feat + 3, cols]
        own_low = oq8[OWN_SLOT, :, cols] * send_buf[feat + 2 : feat + 3, cols]
        out_ref[:, cols] = sums[0:16] + sums[16:32] + low + own_low

    for k in range(STEPS):
        return_copy(k).wait_recv()
    for c in range(nc):
        cols = slice(c * T, (c + 1) * T)
        result = out_ref[:, cols]
        for k in range(STEPS):
            result = result + ret_recv[k, :, cols]
        out_ref[:, cols] = result
    for k in range(STEPS):
        block_copy(send_buf, k, partner, 0).wait_send()
        return_copy(k).wait_send()


def per_device(n, points, values, inverse_scale):
    rhs, pts = values.shape
    vmem = pl.BlockSpec(memory_space=pltpu.VMEM)
    return pl.pallas_call(
        functools.partial(body, n),
        out_shape=jax.ShapeDtypeStruct((rhs, pts), f32),
        in_specs=[pl.BlockSpec(memory_space=pltpu.SMEM)] + [pl.BlockSpec(memory_space=pl.ANY)] * 2,
        out_specs=vmem,
        scratch_shapes=[
            pltpu.VMEM((32, pts), f32),
            pltpu.VMEM((STEPS, 32, pts), f32),
            pltpu.VMEM((pts, 128), bf16),
            pltpu.VMEM((3, 128, pts), bf16),
            pltpu.VMEM((3, 32, pts), bf16),
            pltpu.VMEM((3, 32, pts), f8),
            pltpu.VMEM((T, pts), f32),
            pltpu.VMEM((T, pts), bf16),
            pltpu.VMEM((T, pts), f8),
            pltpu.VMEM((T, pts), bf16),
            pltpu.VMEM((T, pts), f8),
            pltpu.VMEM((4, 32, pts), f32),
            pltpu.VMEM((4, 16, pts), f32),
            pltpu.VMEM((32, pts), f32),
            pltpu.VMEM((16, pts), f32),
            pltpu.VMEM((STEPS, rhs, pts), f32),
            pltpu.VMEM((STEPS, rhs, pts), f32),
            pltpu.VMEM(points.shape, f32),
            pltpu.VMEM(values.shape, f32),
            pltpu.SemaphoreType.DMA((STEPS,)),
            pltpu.SemaphoreType.DMA((STEPS,)),
            pltpu.SemaphoreType.DMA((STEPS,)),
            pltpu.SemaphoreType.DMA((STEPS,)),
            pltpu.SemaphoreType.DMA((2,)),
        ],
        compiler_params=pltpu.CompilerParams(
            collective_id=0, has_side_effects=True, vmem_limit_bytes=48 << 20
        ),
        name="matern",
    )(inverse_scale, points, values)


def solution(mesh):
    placed = (P(None, "blk"), P(None, "blk"), P())
    return jax.shard_map(
        functools.partial(per_device, mesh.shape["blk"]),
        mesh=mesh, in_specs=placed, out_specs=P(None, "blk"), check_vma=False,
    )
```

```python
import functools
import math

import jax
import jax.numpy as jnp
from jax import lax
from jax.experimental import pallas as pl
from jax.experimental.pallas import tpu as pltpu
from jax.sharding import PartitionSpec as P

STEPS = 4
LN2 = math.log(2.0)
SHIFT = 1.5 / LN2
BUMP = 0.75 / LN2**2
FACTOR = LN2**2 / 3.0
POINT_SCALE = math.sqrt(5.0) / LN2
UP = 14
V8_MAX = 240.0
MESH = pl.DeviceIdType.MESH

bf16, f32, f8 = jnp.bfloat16, jnp.float32, jnp.float8_e4m3fn
T = 256
OWN_SLOT, NO_SLOT = 2, 3


def dot(a, b, transposed=False):
    dims = (((1,), (1 if transposed else 0,)), ((), ()))
    return lax.dot_general(a, b, dims, preferred_element_type=f32)


def matern(s):
    s = jnp.maximum(s, 1e-30)
    t = s * lax.rsqrt(s)
    y = t + SHIFT
    return (y * y + BUMP) * jnp.exp2(UP - t)


def parts3(x):
    high = x.astype(bf16).astype(f32)
    rest = x - high
    middle = rest.astype(bf16).astype(f32)
    return high, middle, rest - middle


def body(
    n,
    scale_ref, points_ref, values_ref, out_ref,
    send_buf, recv_buf, home_t, b_ref, v_ref, v8_ref,
    s_ref, kh0, kl0, kh1, kl1, oq, oq8, op, op8, ret_send, ret_recv,
    points_buf, values_buf, send_sem, recv_sem, rsend_sem, rrecv_sem, load_sem,
):
    me = lax.axis_index("blk")
    loads = [
        pltpu.make_async_copy(points_ref, points_buf, load_sem.at[0]),
        pltpu.make_async_copy(values_ref, values_buf, load_sem.at[1]),
    ]
    for load in loads:
        load.start()
    feat, pts = points_ref.shape
    nc = pts // T
    own_steps = nc // 2 + 1
    total = own_steps + STEPS * nc
    first = own_steps
    high_refs, low_refs = (kh0, kh1), (kl0, kl1)

    def ahead(d):
        return lax.rem(me + n - d, n)

    def behind(d):
        return lax.rem(me + d, n)

    odd = 1 - lax.rem(me, 2)
    partner = me - 1 + 2 * odd
    barrier = pltpu.get_barrier_semaphore()
    for other in (ahead(2), partner):
        pl.semaphore_signal(barrier, inc=1, device_id=(other,), device_id_type=MESH)

    for load in loads:
        load.wait()
    norm = jnp.zeros((1, pts), f32)
    for r in range(feat):
        w = points_buf[r : r + 1, :] * (scale_ref[r] * POINT_SCALE)
        send_buf[r : r + 1, :] = w
        norm = norm + w * w
    scaled = values_buf[...] * (FACTOR * 2.0**-UP)
    largest = jnp.max(jnp.max(jnp.abs(scaled), axis=0, keepdims=True), axis=1, keepdims=True)
    send_buf[feat : feat + 1, :] = norm
    send_buf[feat + 1 : feat + 2, :] = jnp.ones((1, pts), f32)
    send_buf[feat + 2 : feat + 3, :] = jnp.broadcast_to(
        jnp.maximum(largest, 1e-30) * (1.0 / V8_MAX), (1, pts)
    )
    send_buf[feat + 3 : 16, :] = jnp.zeros((13 - feat, pts), f32)
    send_buf[16:32, :] = scaled


    def distance(k):
        even_order = jnp.where(k == 0, 1, jnp.where(k == 1, 3, jnp.where(k == 2, 4, 2)))
        odd_order = jnp.where(k == 0, 2, jnp.where(k == 1, 4, jnp.where(k == 2, 3, 1)))
        return jnp.where(odd == 1, odd_order, even_order)

    def block_copy(source, number, target, slot):
        return pltpu.make_async_remote_copy(
            src_ref=source,
            dst_ref=recv_buf.at[slot],
            send_sem=send_sem.at[number],
            recv_sem=recv_sem.at[slot],
            device_id=(target,),
            device_id_type=MESH,
        )

    def first_copy():
        return block_copy(send_buf, 0, behind(2), 3 - 3 * odd)

    def relay(source):
        block_copy(source, 1, behind(2), 2 - odd).start()
        block_copy(source, 2, partner, 3 - 2 * odd).start()

    def arrived(slot):
        block_copy(send_buf, 0, partner, slot).wait_recv()

    def return_copy(k):
        return pltpu.make_async_remote_copy(
            src_ref=ret_send.at[k],
            dst_ref=ret_recv.at[distance(k) - 1],
            send_sem=rsend_sem.at[k],
            recv_sem=rrecv_sem.at[distance(k) - 1],
            device_id=(ahead(distance(k)),),
            device_id_type=MESH,
        )

    pl.semaphore_wait(barrier, 2)

    @pl.when(odd == 1)
    def _():
        first_copy().start()
        block_copy(send_buf, 3, partner, 0).start()

    def prepare(source, slot):
        for c in range(nc):
            cols = slice(c * T, (c + 1) * T)
            high, middle, low = (q.astype(bf16) for q in parts3(source[0:16, cols]))
            for g, part in enumerate((high, middle, high, middle, low, high)):
                b_ref[slot, 16 * g : 16 * g + 16, cols] = part
            v = source[16:32, cols]
            vh = v.astype(bf16)
            v_ref[slot, 0:16, cols] = vh
            v_ref[slot, 16:32, cols] = (v - vh.astype(f32)).astype(bf16)
            v8 = v * (1.0 / source[feat + 2 : feat + 3, cols])
            v8_ref[slot, :, cols] = jnp.concatenate([v8, jnp.zeros_like(v8)], 0).astype(f8)

    row = lax.broadcasted_iota(jnp.int32, (16, T), 0)
    nothing = jnp.zeros((32, T), f32)
    for c in range(nc):
        cols = slice(c * T, (c + 1) * T)
        y = jnp.where(
            row < feat,
            -2.0 * send_buf[0:16, cols],
            jnp.where(row == feat, 1.0, jnp.where(row == feat + 1, send_buf[feat : feat + 1, cols], 0.0)),
        )
        high, middle, low = parts3(y)
        left = jnp.concatenate([high, high, middle, middle, high, low, nothing], 0)
        home_t[cols, :] = left.T.astype(bf16)
    for slot in range(3):
        b_ref[slot, 96:128, :] = jnp.zeros((32, pts), bf16)
    prepare(send_buf, OWN_SLOT)
    for ref in (op, op8, oq, oq8):
        ref[...] = jnp.zeros_like(ref)

    def place(g):
        v = g - first
        visit = jnp.logical_and(v >= 0, v < STEPS * nc)
        k = jnp.clip(v, 0, STEPS * nc - 1) // nc
        own = jnp.where(v < 0, g, g - STEPS * nc)
        slot = jnp.where(visit, lax.rem(k, 2), OWN_SLOT)
        offset = jnp.where(visit, jnp.clip(v, 0, STEPS * nc - 1) - k * nc, own)
        once = jnp.logical_or(own == 0, own == nc // 2)
        sums = jnp.where(visit, lax.rem(k, 2), jnp.where(once, NO_SLOT, OWN_SLOT))
        return slot, offset, sums

    def column(j, offset):
        return pl.ds(pl.multiple_of(lax.rem(j + offset, nc) * T, T), T)

    def cross(where, j):
        slot, offset, _ = where
        s_ref[:, j * T : (j + 1) * T] = dot(
            home_t[j * T : (j + 1) * T, :], b_ref[slot, :, column(j, offset)]
        )

    def elementwise(parity, j):
        for a in range(0, T, 32):
            rows, cols = slice(a, a + 32), slice(j * T, (j + 1) * T)
            k = matern(s_ref[rows, cols])
            high = k.astype(bf16)
            high_refs[parity][rows, cols] = high
            low_refs[parity][rows, cols] = (k - high.astype(f32)).astype(f8)

    def apply(where, parity, j):
        slot, offset, sums = where
        tile, cols = slice(j * T, (j + 1) * T), column(j, offset)
        kh, kl = high_refs[parity][:, tile], low_refs[parity][:, tile]
        op[:, tile] += dot(v_ref[slot, :, cols], kh, True)
        oq[sums, :, cols] += dot(v_ref[OWN_SLOT, :, tile], kh)
        op8[:, tile] += dot(v8_ref[slot, 0:16, cols], kl, True)
        oq8[sums, :, cols] += dot(v8_ref[OWN_SLOT, 0:16, tile], kl)

    def take(k):
        @pl.when(jnp.logical_or(odd == 1, k < 2))
        def _():
            arrived(k)

        @pl.when(jnp.logical_and(odd == 1, k == 0))
        def _():
            relay(recv_buf.at[0])

        prepare(recv_buf.at[k], lax.rem(k, 2))

    def settle(scale):
        op[0:16, :] += op8[...] * scale
        op8[...] = jnp.zeros_like(op8)

    def give_back(k):
        slot = lax.rem(k, 2)
        scale = send_buf[feat + 2 : feat + 3, :]
        ret_send[k] = oq[slot, 0:16, :] + oq[slot, 16:32, :] + oq8[slot] * scale
        return_copy(k).start()
        oq[slot] = jnp.zeros(oq.shape[1:], f32)
        oq8[slot] = jnp.zeros(oq8.shape[1:], f32)
        settle(recv_buf[k, feat + 2 : feat + 3, :])

    def events(g):
        @pl.when(jnp.logical_and(g == 2, odd == 0))
        def _():
            first_copy().start()

        due = g - first + 1

        @pl.when(jnp.logical_and(lax.rem(due, nc) == 0, jnp.logical_and(due >= 0, due < STEPS * nc)))
        def _():
            take(due // nc)

        @pl.when(jnp.logical_and(g == 6, odd == 0))
        def _():
            arrived(3)
            relay(recv_buf.at[3])

        @pl.when(jnp.logical_and(g == 14, odd == 0))
        def _():
            arrived(2)
            block_copy(recv_buf.at[2], 3, partner, 2).start()

        done = g - first - 1

        @pl.when(done == 0)
        def _():
            settle(send_buf[feat + 2 : feat + 3, :])

        @pl.when(jnp.logical_and(lax.rem(done, nc) == 0, done > 0))
        def _():
            give_back(done // nc - 1)

    def work(g, parity):
        before, after = place(g - 1), place(jnp.minimum(g + 1, total - 1))
        for j in range(nc):
            elementwise(parity, j)
            cross(after, j)
            apply(before, 1 - parity, j)

    start, second = place(jnp.int32(0)), place(jnp.int32(1))
    for j in range(nc):
        cross(start, j)
    for j in range(nc):
        elementwise(0, j)
        cross(second, j)
    def pair(h, carry):
        g = 2 * h + 1
        work(g, 1)
        events(g + 1)
        work(g + 1, 0)
        return carry

    lax.fori_loop(0, (total - 1) // 2, pair, 0)
    slot, offset, _ = place(jnp.int32(total - 1))
    last, last_slot = STEPS - 1, (STEPS - 1) % 2
    for j in range(nc):
        tile, cols = slice(j * T, (j + 1) * T), column(j, offset)
        oq[last_slot, :, cols] += dot(v_ref[OWN_SLOT, :, tile], kh0[:, tile])
        oq8[last_slot, :, cols] += dot(v8_ref[OWN_SLOT, 0:16, tile], kl0[:, tile])
    ret_send[last] = (
        oq[last_slot, 0:16, :] + oq[last_slot, 16:32, :] + oq8[last_slot] * send_buf[feat + 2 : feat + 3, :]
    )
    return_copy(last).start()
    for j in range(nc):
        tile, cols = slice(j * T, (j + 1) * T), column(j, offset)
        op[:, tile] += dot(v_ref[slot, :, cols], kh0[:, tile], True)
        op8[:, tile] += dot(v8_ref[slot, 0:16, cols], kl0[:, tile], True)
    for c in range(nc):
        cols = slice(c * T, (c + 1) * T)
        sums = op[:, cols] + oq[OWN_SLOT, :, cols]
        low = op8[:, cols] * recv_buf[last, feat + 2 : feat + 3, cols]
        own_low = oq8[OWN_SLOT, :, cols] * send_buf[feat + 2 : feat + 3, cols]
        out_ref[:, cols] = sums[0:16] + sums[16:32] + low + own_low

    for k in range(STEPS):
        return_copy(k).wait_recv()
    for c in range(nc):
        cols = slice(c * T, (c + 1) * T)
        result = out_ref[:, cols]
        for k in range(STEPS):
            result = result + ret_recv[k, :, cols]
        out_ref[:, cols] = result
    for k in range(STEPS):
        block_copy(send_buf, k, partner, 0).wait_send()
        return_copy(k).wait_send()


def per_device(n, points, values, inverse_scale):
    rhs, pts = values.shape
    vmem = pl.BlockSpec(memory_space=pltpu.VMEM)
    return pl.pallas_call(
        functools.partial(body, n),
        out_shape=jax.ShapeDtypeStruct((rhs, pts), f32),
        in_specs=[pl.BlockSpec(memory_space=pltpu.SMEM)] + [pl.BlockSpec(memory_space=pl.ANY)] * 2,
        out_specs=vmem,
        scratch_shapes=[
            pltpu.VMEM((32, pts), f32),
            pltpu.VMEM((STEPS, 32, pts), f32),
            pltpu.VMEM((pts, 128), bf16),
            pltpu.VMEM((3, 128, pts), bf16),
            pltpu.VMEM((3, 32, pts), bf16),
            pltpu.VMEM((3, 32, pts), f8),
            pltpu.VMEM((T, pts), f32),
            pltpu.VMEM((T, pts), bf16),
            pltpu.VMEM((T, pts), f8),
            pltpu.VMEM((T, pts), bf16),
            pltpu.VMEM((T, pts), f8),
            pltpu.VMEM((4, 32, pts), f32),
            pltpu.VMEM((4, 16, pts), f32),
            pltpu.VMEM((32, pts), f32),
            pltpu.VMEM((16, pts), f32),
            pltpu.VMEM((STEPS, rhs, pts), f32),
            pltpu.VMEM((STEPS, rhs, pts), f32),
            pltpu.VMEM(points.shape, f32),
            pltpu.VMEM(values.shape, f32),
            pltpu.SemaphoreType.DMA((STEPS,)),
            pltpu.SemaphoreType.DMA((STEPS,)),
            pltpu.SemaphoreType.DMA((STEPS,)),
            pltpu.SemaphoreType.DMA((STEPS,)),
            pltpu.SemaphoreType.DMA((2,)),
        ],
        compiler_params=pltpu.CompilerParams(
            collective_id=0, has_side_effects=True, vmem_limit_bytes=63 << 20
        ),
        name="matern",
    )(inverse_scale, points, values)


def solution(mesh):
    placed = (P(None, "blk"), P(None, "blk"), P())
    return jax.shard_map(
        functools.partial(per_device, mesh.shape["blk"]),
        mesh=mesh, in_specs=placed, out_specs=P(None, "blk"), check_vma=False,
    )
```
